512 devices in a mesh: span: 8 (over x, core), dom: 64 (over y, z).
Axes of the slice: x: 4, y: 4, z: 16, core: 2. Of those that a mesh axis runs over, the one named last changes fastest.
Arguments:
- krylov: float32 [20, 5, 32, 16384], P(None, None, 'span', 'dom'), may hold values from -75 to 75
- limiter: float32 [5, 32, 16384], P(None, 'span', 'dom'), may hold values from 0 to 1
- pseudo_diag: float32 [32, 16384], P('span', 'dom'), may hold values from 1 to 4
- face_states: float32 [2, 5, 32, 32768], P(None, None, 'span', 'dom'), may hold values from -2 to 13.5, as said below
- face_angle: float32 [32768], P('dom'), may hold values from -3.140625 to 3.140625
- face_area: float32 [32768], P('dom'), may hold values from 0.3 to 1.5
- slope_weight: float32 [32768], P('dom'), may hold values from 0.05 to 0.3
- span_coupling: float32 [16384], P('dom'), may hold values from 0.2 to 1
- face_cells: int32 [2, 32768], P(None, 'dom'), may hold values from 0 to 767, as said below
- send_list: int32 [4, 8192], P(None, 'dom'), may hold values from 0 to 255, as said below
- send_count: int32 [4, 64], P(None, 'dom'), may hold values from 0 to 128, as said below
Outputs:
- new_vectors: float32 [3, 5, 32, 16384], P(None, None, 'span', 'dom')
- hessenberg: float32 [3, 23], replicated
The draws below stay inside these ranges and needn't reach their ends.
Inputs may be any that keep to these rules, and one draw needn't show every extreme that they name: `face_cells`: row 0 names owned cells, below 256. A row 1 entry at or above 256 is a ghost slot 256 + j * 128 + k that is live: its sender block exists and k is below that sender's send_count; every live slot of a block is named by exactly one face; a row 1 entry below 256 differs from row 0. `send_list`: entries of one peer slot's list of one block are distinct owned cells. `send_count`: A slot whose receiving block (dom index plus its offset) does not exist has count 0; some block sends a full 128 in slots 2 and 3. `face_states`: each saved state has density and pressure 0.5 or more.
All inputs are finite; a program needn't handle non-finite values.
Results may differ from the reference program's by a relative error of at most 0.00085.
Values sent between devices are 32-bit elements; how exact they have to be, the bound alone decides.
A program may use at most 64 MiB of HBM per device.

```python
import math
import jax
import jax.numpy as jnp
from jax import lax

K = 20
PRODUCTS = 3
CAP = 128
C = 256
NL = 32
PLANE = 16384
FACES = 32768
N_DOM = 64


OFFSET_LIST = (-2, -1, 1, 2)


def topology(key):
    blocks = PLANE // C
    base = jax.random.fold_in(key, 7103)
    keys_all = jax.random.split(base, 6)
    offsets = jnp.array(OFFSET_LIST, jnp.int32)
    device_ids = jnp.arange(blocks, dtype=jnp.int32)
    targets = device_ids[None, :] + offsets[:, None]
    usable = ((targets >= 0) & (targets < blocks)).astype(jnp.int32)
    counts = jax.random.randint(keys_all[0], (4, blocks), CAP // 8, CAP + 1, dtype=jnp.int32) * usable
    chosen = jax.random.randint(keys_all[1], (), 0, blocks - 2, dtype=jnp.int32)
    counts = counts.at[3, chosen].set(CAP).at[2, chosen].set(CAP)
    list_keys = jax.random.split(keys_all[2], 4 * blocks)
    lists = jax.vmap(lambda one_key: jax.random.permutation(one_key, C)[:CAP])(list_keys)
    lists = lists.reshape(4, blocks, CAP).astype(jnp.int32)
    ramp = jnp.arange(CAP, dtype=jnp.int32)
    lists = lists.at[0, 0].set(C - 1 - ramp).at[1, 0].set(ramp)
    per_dev = 2 * C
    owner_cell = jax.random.randint(keys_all[3], (blocks, per_dev), 0, C, dtype=jnp.int32)
    owner_cell = owner_cell.at[0, 0].set(0)
    interior = (owner_cell + jax.random.randint(keys_all[4], (blocks, per_dev), 1, C, dtype=jnp.int32)) % C
    positions = jnp.arange(per_dev, dtype=jnp.int32)
    peer_slot = jnp.minimum(positions // CAP, 3)
    entry_idx = positions % CAP
    sender = device_ids[:, None] - offsets[peer_slot][None, :]
    clipped = jnp.clip(sender, 0, blocks - 1)
    live_count = counts[peer_slot[None, :], clipped]
    used = (positions[None, :] < 4 * CAP) & (sender >= 0) & (sender < blocks) & (entry_idx[None, :] < live_count)
    other_cell = jnp.where(used, C + positions[None, :], interior).astype(jnp.int32)
    face_pairs = jnp.stack([owner_cell, other_cell]).reshape(2, blocks * per_dev)
    return (face_pairs, lists.reshape(4, blocks * CAP), counts)


def draw_face_cells(key, part):
    return topology(key)[0]


def draw_send_list(key, part):
    return topology(key)[1]


def draw_send_count(key, part):
    return topology(key)[2]


def draw_krylov(key, part):
    keys_all = jax.random.split(jax.random.fold_in(key, 311), 4)
    blocks = PLANE // C
    noise = jax.random.truncated_normal(keys_all[0], -4.0, 4.0, (K, 5, NL, PLANE), jnp.float32)
    shared = jax.random.truncated_normal(keys_all[1], -4.0, 4.0, (5, NL, PLANE), jnp.float32)
    weights = jax.random.uniform(keys_all[2], (K, 1, 1, 1), jnp.float32, 0.5, 1.5)
    rising = 1.0 + 2.0 * (jnp.arange(PLANE) // C).astype(jnp.float32) / max(blocks - 1, 1)
    scales = jnp.ones((1, 5, 1, 1), jnp.float32)
    mixing = 0.6
    return rising * scales * (0.8 * noise + mixing * weights * shared)


def draw_face_states(key, part):
    keys_all = jax.random.split(jax.random.fold_in(key, 523), 5)
    dims = (2, NL, FACES)
    density = jax.random.uniform(keys_all[0], dims, jnp.float32, 0.6, 1.6)
    vel_x = jax.random.uniform(keys_all[1], dims, jnp.float32, 0.2, 2.4)
    pressure = jax.random.uniform(keys_all[4], dims, jnp.float32, 0.6, 2.2)
    vel_y = jnp.clip(0.4 * jax.random.normal(keys_all[2], dims, jnp.float32), -1.0, 1.0)
    vel_z = jnp.clip(0.2 * jax.random.normal(keys_all[3], dims, jnp.float32), -0.5, 0.5)
    energy = pressure / 0.4 + 0.5 * density * (vel_x * vel_x + vel_y * vel_y + vel_z * vel_z)
    return jnp.stack([density, density * vel_x, density * vel_y, density * vel_z, energy], axis=1)


def steps_of(rng, shape, shards, least, top_value):
    loudness, own = 1.0, jax.random.fold_in(rng, 6)
    for dim, shards_of in shards:
        draws = jnp.exp(jax.random.uniform(jax.random.fold_in(own, dim), (shards_of,), jnp.float32, least / len(shards), top_value / len(shards)))
        loudness = loudness * jnp.repeat(draws, shape[dim] // shards_of).reshape([-1 if axis == dim else 1 for axis in range(len(shape))])
    return loudness


def setup_inputs(seed: int = 0) -> dict:
    key_list = jax.random.split(jax.random.key(seed), 12)
    return {
        "krylov": draw_krylov(jax.random.fold_in(key_list[11], 71), 0),
        "limiter": jnp.clip(1.0 * jax.random.uniform(key_list[1], (5, NL, PLANE), jnp.float32) ** steps_of(key_list[1], (5, NL, PLANE), ((1, 8), (2, 64)), -0.2, 0.2), 0.0, 1.0),
        "pseudo_diag": jnp.clip(1.0 + 3.0 * jax.random.uniform(key_list[2], (NL, PLANE), jnp.float32) ** steps_of(key_list[2], (NL, PLANE), ((0, 8), (1, 64)), -0.2, 0.2), 1.0, 4.0),
        "face_states": draw_face_states(jax.random.fold_in(key_list[11], 71), 0),
        "face_angle": jnp.clip(jax.random.uniform(key_list[4], (FACES,), jnp.float32, -3.140625, 3.140625), -3.140625, 3.140625),
        "face_area": jnp.clip(jnp.exp(math.log(1.5) - 1.60943787 * jax.random.uniform(key_list[5], (FACES,), jnp.float32) ** steps_of(key_list[5], (FACES,), ((0, 64),), -0.2, 0.2)), 0.3, 1.5),
        "slope_weight": jnp.clip(jnp.exp(math.log(0.3) - 1.7917595 * jax.random.uniform(key_list[6], (FACES,), jnp.float32) ** steps_of(key_list[6], (FACES,), ((0, 64),), -0.2, 0.2)), 0.05, 0.3),
        "span_coupling": jnp.clip(jnp.exp(math.log(1.0) - 1.609438 * jax.random.uniform(key_list[7], (PLANE,), jnp.float32) ** steps_of(key_list[7], (PLANE,), ((0, 64),), -0.2, 0.2)), 0.2, 1.0),
        "face_cells": draw_face_cells(jax.random.fold_in(key_list[11], 71), 0),
        "send_list": draw_send_list(jax.random.fold_in(key_list[11], 71), 0),
        "send_count": draw_send_count(jax.random.fold_in(key_list[11], 71), 0),
    }


OFFSET_LIST = (-2, -1, 1, 2)
EPSILON = 1e-06

def normal_flux(state_in, normal_x, normal_y):
    density = state_in[0]
    vel_x = state_in[1] / density
    vel_y = state_in[2] / density
    vel_z = state_in[3] / density
    pressure = 0.4 * (state_in[4] - 0.5 * (state_in[1] * vel_x + state_in[2] * vel_y + state_in[3] * vel_z))
    normal_vel = vel_x * normal_x + vel_y * normal_y
    flux_out = jnp.stack([state_in[0] * normal_vel, state_in[1] * normal_vel + pressure * normal_x, state_in[2] * normal_vel + pressure * normal_y, state_in[3] * normal_vel, (state_in[4] + pressure) * normal_vel])
    wave_speed = jnp.abs(normal_vel) + jnp.sqrt(1.4 * pressure / density)
    return (flux_out, wave_speed)

def face_flux(left_state, right_state, normal_x, normal_y, face_area):
    flux_left, speed_left = normal_flux(left_state, normal_x, normal_y)
    flux_right, speed_right = normal_flux(right_state, normal_x, normal_y)
    wave_bound = lax.stop_gradient(jnp.maximum(speed_left, speed_right))
    return face_area * (0.5 * (flux_left + flux_right) - 0.5 * wave_bound * (right_state - left_state))

def flux_transpose(states, normal_x, normal_y, face_area, cotangent):

    def applied(left_in, right_in):
        return face_flux(left_in, right_in, normal_x, normal_y, face_area)
    _, pullback = jax.vjp(applied, states[0], states[1])
    return pullback(cotangent)

def prepare(face_cells, send_list, send_count):
    per_dev = 2 * C
    face_total = face_cells.shape[1]
    device = jnp.arange(face_total, dtype=jnp.int32) // per_dev
    owner_cell = device * C + face_cells[0]
    local_idx = face_cells[1]
    ghost_slot = jnp.maximum(local_idx - C, 0)
    peer_slot = jnp.minimum(ghost_slot // CAP, 3)
    entry_idx = ghost_slot % CAP
    offsets = jnp.array(OFFSET_LIST, jnp.int32)
    sender = device - offsets[peer_slot]
    clipped = jnp.clip(sender, 0, N_DOM - 1)
    live = (sender >= 0) & (sender < N_DOM) & (entry_idx < send_count[peer_slot, clipped])
    remote = clipped * C + send_list[peer_slot, clipped * CAP + entry_idx]
    is_local = local_idx < C
    other_cell = jnp.where(is_local, device * C + local_idx, remote).astype(jnp.int32)
    live_weight = jnp.where(is_local | live, 1.0, 0.0).astype(jnp.float32)
    return (owner_cell.astype(jnp.int32), other_cell, live_weight)

def transposed_apply(vector, limiter, pseudo_diag, face_states, normal_x, normal_y, face_area, slope_weight, span_coupling, owner_cell, other_cell, live_weight):

    def layer_terms(inputs):
        values, states, limits = inputs
        jump_vals = values[:, owner_cell] - live_weight * values[:, other_cell]
        adj_left, adj_right = flux_transpose(states, normal_x, normal_y, face_area, jump_vals)
        state_part = jnp.zeros(values.shape, jnp.float32).at[:, owner_cell].add(adj_left)
        state_part = state_part.at[:, other_cell].add(live_weight * adj_right)
        slope_adj = limits * state_part
        moved = slope_weight * (slope_adj[:, owner_cell] - live_weight * slope_adj[:, other_cell])
        slope_part = jnp.zeros(values.shape, jnp.float32).at[:, owner_cell].add(-moved)
        slope_part = slope_part.at[:, other_cell].add(live_weight * moved)
        return state_part + slope_part
    stacked = lax.map(layer_terms, (jnp.moveaxis(vector, 1, 0), jnp.moveaxis(face_states, 2, 0), jnp.moveaxis(limiter, 1, 0)))
    face_terms = jnp.moveaxis(stacked, 0, 1)
    spanwise = span_coupling * (2.0 * vector - jnp.roll(vector, 1, axis=1) - jnp.roll(vector, -1, axis=1))
    return pseudo_diag * vector + spanwise + face_terms

def reference(krylov, limiter, pseudo_diag, face_states, face_angle, face_area, slope_weight, span_coupling, face_cells, send_list, send_count):
    dense_reference = lax.Precision.HIGHEST
    owner_cell, other_cell, live_weight = prepare(face_cells, send_list, send_count)
    normal_x = jnp.cos(face_angle)
    normal_y = jnp.sin(face_angle)
    count_all = 5 * NL * PLANE
    krylov_dimension = krylov.shape[0]
    gram = jnp.einsum('kvlc,jvlc->kj', krylov, krylov, precision=dense_reference) / count_all
    factor = jnp.linalg.cholesky(gram)
    vectors = []
    hess_rows = []
    current = krylov[krylov_dimension - 1]
    for number in range(PRODUCTS):
        adjoint_output = transposed_apply(current, limiter, pseudo_diag, face_states, normal_x, normal_y, face_area, slope_weight, span_coupling, owner_cell, other_cell, live_weight)
        partition_sums = jnp.einsum('zbis,bis->z', krylov, adjoint_output, precision=dense_reference)
        if vectors:
            extra_sums = jnp.stack([jnp.sum(finished * adjoint_output) for finished in vectors])
            partition_sums = jnp.concatenate([partition_sums, extra_sums])
        projected_vector = partition_sums / count_all
        solved = jax.scipy.linalg.cho_solve((factor, True), projected_vector[:krylov_dimension])
        hessenberg_column = jnp.concatenate([solved, projected_vector[krylov_dimension:]])
        residual_piece = adjoint_output - jnp.einsum('p,pohz->ohz', hessenberg_column[:krylov_dimension], krylov, precision=dense_reference)
        for position, finished in enumerate(vectors):
            residual_piece = residual_piece - hessenberg_column[krylov_dimension + position] * finished
        scale_norm = jnp.sqrt(jnp.sum(residual_piece * residual_piece) / count_all + EPSILON)
        current = residual_piece / scale_norm
        vectors.append(current)
        hess_rows.append(jnp.concatenate([hessenberg_column, jnp.zeros((krylov_dimension + PRODUCTS - 1 - hessenberg_column.shape[0],), jnp.float32), jnp.reshape(scale_norm, (1,))]))
    return (jnp.stack(vectors), jnp.stack(hess_rows))
```

```python
import functools

import jax
import jax.numpy as jnp
from jax import lax
from jax.experimental import pallas as pl
from jax.experimental.pallas import tpu as pltpu
from jax.sharding import PartitionSpec as P

MESH = pl.DeviceIdType.MESH
OFFSETS = (-2, -1, 1, 2)
NEAR = (1, 2, 0, 3)
EPSILON = 1e-06
F32 = jnp.float32
BF16 = jnp.bfloat16
STEPS = 3
NVEC = 20
CELLS = 256
FACES = 512
CAP = 128


def dot_nn(a, b):
    return lax.dot_general(a, b, (((1,), (0,)), ((), ())), preferred_element_type=F32)


def dot_nt(a, b):
    return lax.dot_general(a, b, (((1,), (1,)), ((), ())), preferred_element_type=F32)


def iota(shape, dim):
    return lax.broadcasted_iota(jnp.int32, shape, dim)


def top_rows(shape):
    return (iota(shape, 0) & 4) == 0


def flip(x):
    return pltpu.roll(x, 4, 0)


def split2(x):
    hi = x.astype(BF16).astype(F32)
    return jnp.concatenate([hi, x - hi], axis=0)


def split3(x):
    hi = x.astype(BF16).astype(F32)
    rest = x - hi
    mid = rest.astype(BF16).astype(F32)
    return jnp.concatenate([hi, mid, rest - mid], axis=0)


def operand(fields):
    both = split2(jnp.concatenate(fields, axis=0))
    top = top_rows(both.shape)
    return jnp.concatenate([jnp.where(top, both, 0.0), jnp.where(top, 0.0, both)], axis=1).astype(BF16)


def joined(y):
    half = y.shape[0] // 2
    return y[:half] + y[half:]


def packed_cells(y):
    out = []
    for v in range(5):
        low, high = y[8 * v : 8 * v + 8, :CAP], y[8 * v : 8 * v + 8, CAP:]
        top = top_rows(low.shape)
        out.append(jnp.where(top, low, high) + flip(jnp.where(top, high, low)))
    return out


def one_hot(size, row):
    return (iota((size, row.shape[1]), 0) == row).astype(F32)


def kernel(
    grid,
    count,
    k_any,
    lim_any,
    pd_any,
    fs_any,
    pack_any,
    sl_any,
    nv_any,
    hess_ref,
    kv,
    limv,
    pdv,
    fsv,
    packv,
    slv,
    nvs,
    sv,
    rv,
    w_own,
    w_sc,
    w_nb,
    cf_int,
    cf_gf,
    pl_int,
    pl_gf,
    msg_out,
    msg_in,
    nbuf,
    sbuf,
    gbuf,
    abuf,
    load_sem,
    out_sem,
    msg_send,
    msg_recv,
    nb_send,
    nb_recv,
    sp_send,
    sp_recv,
    g_send,
    g_recv,
    a_send,
    a_recv,
):
    ns, ny, nz = grid
    nd = ny * nz
    s = lax.axis_index("span")
    d = lax.axis_index("dom")
    y, z = d // nz, lax.rem(d, nz)

    def dom_at(offset):
        return lax.rem(d + (offset + nd), nd)

    def span_at(offset):
        return lax.rem(s + (offset + ns), ns)

    groups = (
        (ns, s, lambda t: (t, d)),
        (ny, y, lambda t: (s, t * nz + z)),
        (nz, z, lambda t: (s, y * nz + t)),
    )
    starts = (0, ns, ns + ny)

    loads = [
        pltpu.make_async_copy(src, dst, load_sem.at[i])
        for i, (src, dst) in enumerate(
            (
                (pack_any, packv),
                (fs_any, fsv),
                (sl_any, slv),
                (k_any, kv),
                (lim_any, limv),
                (pd_any, pdv),
            )
        )
    ]
    for load in loads:
        load.start()

    barrier = pltpu.get_barrier_semaphore()
    partners = 0
    for o in OFFSETS:
        pl.semaphore_signal(barrier, inc=1, device_id=(s, dom_at(o)), device_id_type=MESH)
        partners += 1
    for n, me, device in groups:
        for k in range(1, n):
            pl.semaphore_signal(barrier, inc=1, device_id=device(lax.rem(me + k, n)), device_id_type=MESH)
            partners += 1

    def send_field(src, number):
        copies = []
        for j in NEAR:
            copy = pltpu.make_async_remote_copy(
                src_ref=src,
                dst_ref=nbuf.at[number, 3 - j],
                send_sem=nb_send.at[number, j],
                recv_sem=nb_recv.at[number, 3 - j],
                device_id=(s, dom_at(OFFSETS[j])),
                device_id_type=MESH,
            )
            copy.start()
            copies.append((j, copy))
        return dict(copies)

    def send_span(src, number):
        copies = []
        for side, offset in ((0, 1), (1, -1)):
            copy = pltpu.make_async_remote_copy(
                src_ref=src,
                dst_ref=sbuf.at[number, side],
                send_sem=sp_send.at[number, side],
                recv_sem=sp_recv.at[number, side],
                device_id=(span_at(offset), d),
                device_id_type=MESH,
            )
            copy.start()
            copies.append(copy)
        return copies

    unsent = []

    def sum_start(buf, send, recv, stage, value):
        n, me, device = groups[stage]
        buf[pl.ds(starts[stage] + me, 1)] = value[None]
        for k in range(1, n):
            place = buf.at[starts[stage] + me]
            pltpu.make_async_remote_copy(
                src_ref=place,
                dst_ref=place,
                send_sem=send.at[stage],
                recv_sem=recv.at[stage],
                device_id=device(lax.rem(me + k, n)),
                device_id_type=MESH,
            ).start()
        span = buf.at[pl.ds(starts[stage], n - 1)]
        unsent.append(pltpu.make_async_copy(span, span, send.at[stage]))

    def sum_finish(buf, recv, stage):
        n = groups[stage][0]
        span = buf.at[pl.ds(starts[stage], n - 1)]
        pltpu.make_async_copy(span, span, recv.at[stage]).wait()
        total = buf[starts[stage]]
        for k in range(1, n):
            total = total + buf[starts[stage] + k]
        return total

    loads[0].wait()
    loads[1].wait()
    angle, area, weight = packv[0:1, :], packv[1:2, :], packv[2:3, :]
    owner = packv[3:4, :].astype(jnp.int32)
    other = packv[4:5, :].astype(jnp.int32)
    nx, ny_ = jnp.cos(angle), jnp.sin(angle)
    state = [jnp.concatenate([fsv[0, v], fsv[1, v]], axis=0) for v in range(5)]
    inv = 1.0 / state[0]
    u1, u2, u3 = state[1] * inv, state[2] * inv, state[3] * inv
    pressure = 0.4 * (state[4] - 0.5 * (state[1] * u1 + state[2] * u2 + state[3] * u3))
    enthalpy = (state[4] + pressure) * inv
    speed = jnp.abs(u1 * nx + u2 * ny_) + jnp.sqrt(1.4 * pressure * inv)
    lam = jnp.maximum(speed, flip(speed))
    lam = jnp.where(top_rows(lam.shape), lam, -lam)
    half_area = 0.5 * area
    coefs = [u1, u2, u3, enthalpy, lam]
    for i, c in enumerate(coefs):
        cf_int[i] = c
    inside = (other < CELLS).astype(F32)
    pl_int[0:1, :] = nx
    pl_int[1:2, :] = ny_
    pl_int[2:3, :] = half_area * inside
    pl_int[3:4, :] = weight * inside
    pl_int[4:8, :] = jnp.zeros((4, FACES), F32)

    loads[2].wait()
    plane_rows = jnp.concatenate(
        [nx, ny_, half_area, weight, packv[3:4, :], jnp.zeros((3, FACES), F32)], axis=0
    )
    gathered = split3(jnp.concatenate([*coefs, plane_rows], axis=0)).astype(BF16)
    for j in range(4):
        slots = (iota((CAP, FACES), 0) + (CELLS + j * CAP) == other).astype(F32).astype(BF16)
        part = dot_nt(gathered, slots)
        part = part[0:48] + part[48:96] + part[96:144]
        msg_out[j, 0:45, :] = part[0:45]
        msg_out[j, 45:46, :] = slv[3 - j : 4 - j, :].astype(F32)
        msg_out[j, 46:48, :] = jnp.zeros((2, CAP), F32)

    loads[3].wait()
    pl.semaphore_wait(barrier, partners)

    first = send_field(kv.at[pl.ds(40 * NVEC - 40, 40)], 0)
    messages = {}
    for j in NEAR:
        copy = pltpu.make_async_remote_copy(
            src_ref=msg_out.at[j],
            dst_ref=msg_in.at[j],
            send_sem=msg_send.at[j],
            recv_sem=msg_recv.at[j],
            device_id=(s, dom_at(-OFFSETS[j])),
            device_id_type=MESH,
        )
        copy.start()
        messages[j] = copy
    first_span = send_span(kv.at[pl.ds(40 * NVEC - 40, 40)], 0)

    total = jnp.zeros((72, 72), F32)
    for pair in range(20):
        rows = jnp.concatenate(
            [kv[pl.ds(2 * pair + i, NVEC, stride=40), :] for i in range(2)], axis=1
        )
        rows = jnp.concatenate([rows, jnp.zeros((4, 2 * CAP), F32)], axis=0)
        rows = split3(rows).astype(BF16)
        total = total + dot_nt(rows, rows)
    rows = total[0:24] + total[24:48] + total[48:72]
    gram = rows[:, 0:24] + rows[:, 24:48] + rows[:, 48:72]
    gram = jnp.concatenate([gram, jnp.zeros((24, CAP - 24), F32)], axis=1)
    gram = gram[0:8] + pltpu.roll(gram[8:16], 32, 1) + pltpu.roll(gram[16:24], 64, 1)
    sum_start(gbuf, g_send, g_recv, 0, gram)

    hot_a, hot_b = one_hot(CELLS, owner), one_hot(CELLS, other)
    w_own[:, 0:512] = (hot_a - hot_b).astype(BF16)
    w_sc[:, 0:512] = hot_a.astype(BF16)
    w_sc[:, 512:1024] = hot_b.astype(BF16)
    for j in range(4):
        at = 512 + j * CAP
        hot = one_hot(CELLS, msg_out[j, 44:45, :].astype(jnp.int32)).astype(BF16)
        w_own[:, at : at + CAP] = hot
        w_sc[:, at + 512 : at + 512 + CAP] = hot
        hot = one_hot(CELLS, slv[j : j + 1, :])
        w_own[:, at + 512 : at + 512 + CAP] = (-hot).astype(BF16)
        w_sc[:, at + 1024 : at + 1024 + CAP] = hot.astype(BF16)

    gram = sum_finish(gbuf, g_recv, 0)
    sum_start(gbuf, g_send, g_recv, 1, gram)

    for j in NEAR:
        messages[j].wait_recv()
        at = j * CAP
        for i in range(5):
            mine, theirs = msg_out[j, 8 * i : 8 * i + 8, :], msg_in[j, 8 * i : 8 * i + 8, :]
            cf_gf[i, :, at : at + CAP] = jnp.where(top_rows(mine.shape), mine, theirs)
        for side, msg in ((0, msg_out), (1, msg_in)):
            pl_gf[side, :, at : at + CAP] = msg[j, 40:48, :]
        w_nb[j, :, 0:CAP] = (-one_hot(CELLS, msg_in[j, 45:46, :].astype(jnp.int32))).astype(BF16)
        w_nb[j, :, CAP:] = one_hot(CELLS, msg_in[j, 44:45, :].astype(jnp.int32)).astype(BF16)

    def jumps(own, number, copies):
        near = joined(dot_nn(operand(own), w_own[...]))
        ghost = [None] * 4
        foreign = [None] * 4
        for j in NEAR:
            copies[3 - j].wait_recv()
            part = joined(dot_nn(operand([nbuf[number, j]]), w_nb[j]))
            ghost[3 - j] = part[:, :CAP]
            foreign[j] = part[:, CAP:]
        return (
            near[:, 0:512],
            near[:, 512:1024] + jnp.concatenate(ghost, axis=1),
            near[:, 1024:1536] + jnp.concatenate(foreign, axis=1),
        )

    def transposed(e, cf, nx, ny, half_area):
        e = [half_area * x for x in e]
        u1, u2, u3, enthalpy, lam = (cf[i] for i in range(5))
        vn = u1 * nx + u2 * ny
        phi = 0.2 * (u1 * u1 + u2 * u2 + u3 * u3)
        cp = e[1] * nx + e[2] * ny + e[4] * vn
        ch = e[0] + e[1] * u1 + e[2] * u2 + e[3] * u3 + e[4] * enthalpy
        diag = vn + lam
        cp4 = 0.4 * cp
        return [
            e[0] * diag + cp * phi - ch * vn,
            e[1] * diag - u1 * cp4 + ch * nx,
            e[2] * diag - u2 * cp4 + ch * ny,
            e[3] * diag - u3 * cp4,
            e[4] * diag + cp4,
        ]

    def state_part(own, number, copies):
        e_int, e_gh, e_for = jumps(own, number, copies)
        jump_int, jump_gf = [], []
        for v in range(5):
            x = e_int[8 * v : 8 * v + 8]
            jump_int.append(x + flip(x))
            g, f = e_gh[8 * v : 8 * v + 8], e_for[8 * v : 8 * v + 8]
            top = top_rows(g.shape)
            jump_gf.append(jnp.where(top, g, f) + flip(jnp.where(top, f, g)))
        g_int = transposed(jump_int, cf_int, pl_int[0:1, :], pl_int[1:2, :], pl_int[2:3, :])
        top = top_rows((8, FACES))
        rows = [jnp.where(top, pl_gf[0, i : i + 1, :], pl_gf[1, i : i + 1, :]) for i in range(3)]
        g_gf = transposed(jump_gf, cf_gf, *rows)
        parts = []
        for g in (jnp.concatenate(g_int, axis=0), jnp.concatenate(g_gf, axis=0)):
            top = top_rows(g.shape)
            parts += [jnp.where(top, g, 0.0), jnp.where(top, 0.0, g)]
        lhs = split2(jnp.concatenate(parts, axis=1)).astype(BF16)
        return packed_cells(joined(dot_nt(lhs, w_sc[...])))

    def slope_part(own, number, copies):
        d_int, d_gh, d_for = jumps(own, number, copies)
        lhs = jnp.concatenate(
            [d_int * pl_int[3:4, :], d_gh * pl_gf[0, 3:4, :], d_for * pl_gf[1, 3:4, :]], axis=1
        )
        return packed_cells(joined(dot_nt(split2(lhs).astype(BF16), w_own[...])))

    row = iota((8, CAP), 0)
    layer = row & 3
    coupling = jnp.where(row < 4, packv[5:6, 0:CAP], packv[5:6, CAP : 2 * CAP])
    eye = iota((24, CAP), 0) == iota((24, CAP), 1)
    row24 = iota((24, CAP), 0)

    def row_of(column):
        return jnp.sum(jnp.where(eye, column, 0.0), axis=0, keepdims=True)

    def local_sums(terms):
        rows = []
        for i in range(24):
            if i in terms:
                rows.append(jnp.sum(terms[i], axis=0, keepdims=True))
            else:
                rows.append(jnp.zeros((1, CAP), F32))
        return row_of(jnp.sum(jnp.concatenate(rows, axis=0), axis=1, keepdims=True))

    def product(a, b):
        out = a[0] * b[0]
        for v in range(1, 5):
            out = out + a[v] * b[v]
        return out

    def basis(i):
        return [kv[40 * i + 8 * v : 40 * i + 8 * v + 8, :] for v in range(5)]

    q = basis(NVEC - 1)
    copies, span_copies = first, first_span
    inverse = None
    done = []
    rr = None
    hess = []
    for m in range(STEPS):
        state_terms = state_part(q, 2 * m, copies)
        if m == 0:
            gram = sum_finish(gbuf, g_recv, 1)
            sum_start(gbuf, g_send, g_recv, 2, gram)
            loads[4].wait()
            loads[5].wait()
        slope_field = [limv[v] * state_terms[v] for v in range(5)]
        sv[m] = jnp.concatenate(slope_field, axis=0)
        slope_copies = send_field(sv.at[m], 2 * m + 1)
        for copy in span_copies:
            copy.wait_recv()
        local = []
        for v in range(5):
            above = jnp.where(layer == 0, pltpu.roll(sbuf[m, 0, 8 * v : 8 * v + 8, :], 5, 0), pltpu.roll(q[v], 1, 0))
            below = jnp.where(layer == 3, pltpu.roll(sbuf[m, 1, 8 * v : 8 * v + 8, :], 3, 0), pltpu.roll(q[v], 7, 0))
            local.append(
                pdv[...] * q[v] + coupling * (2.0 * q[v] - above - below) + state_terms[v]
            )
        if m == 0:
            gram = sum_finish(gbuf, g_recv, 2) / count
            wide = jnp.concatenate(
                [gram, pltpu.roll(gram, CAP - 32, 1), pltpu.roll(gram, CAP - 64, 1)], axis=0
            )
            lane = iota((24, CAP), 1)
            kept = (lane < NVEC) & (row24 < NVEC)
            diagonal = (row24 == lane) & (row24 >= NVEC)
            work = jnp.where(kept, wide, 0.0) + jnp.where(diagonal | (lane == row24 + 32), 1.0, 0.0)
            for k in range(NVEC):
                column = jnp.sum(jnp.where(lane == k, work, 0.0), axis=1, keepdims=True)
                pivot = work[k : k + 1, :]
                scale = 1.0 / column[k : k + 1, :]
                work = work - (column - jnp.where(row24[:, 0:1] == k, 1.0, 0.0)) * (pivot * scale)
            inverse = pltpu.roll(work, CAP - 32, 1)
        slope_terms = slope_part(slope_field, 2 * m + 1, slope_copies)
        w = [local[v] - slope_terms[v] for v in range(5)]

        terms = {i: product(basis(i), w) for i in range(NVEC)}
        for i, vector in enumerate(done):
            terms[NVEC + i] = product(vector, w)
        if m:
            terms[NVEC + m - 1] = product(q, w)
            terms[22] = rr
        value = local_sums(terms)
        for stage in range(3):
            sum_start(abuf.at[m], a_send.at[m], a_recv.at[m], stage, value)
            value = sum_finish(abuf.at[m], a_recv.at[m], stage)
        solved = jnp.sum(inverse * (value / count), axis=1, keepdims=True)
        if m:
            beta = jnp.sqrt(solved[22:23, :] + EPSILON)
            scale = 1.0 / beta
            last = [x * scale for x in q]
            nvs[m - 1] = jnp.concatenate(last, axis=0)
            pltpu.make_async_copy(nvs.at[m - 1], nv_any.at[m - 1], out_sem.at[m - 1]).start()
            done.append(last)
            hess[-1] = jnp.where(iota((1, CAP), 1) == 22, beta, hess[-1])
            w = [x * scale for x in w]
            solved = solved * scale
            solved = jnp.where(row24[:, 0:1] == NVEC + m - 1, solved * scale, solved)
        hess.append(jnp.where(iota((1, CAP), 1) < NVEC + m, row_of(solved), 0.0))
        wide = jnp.broadcast_to(solved, (24, CAP))
        r = w
        for i in range(NVEC + m):
            c = wide[i : i + 1, :]
            vector = basis(i) if i < NVEC else done[i - NVEC]
            r = [r[v] - c * vector[v] for v in range(5)]
        rv[m] = jnp.concatenate(r, axis=0)
        if m + 1 < STEPS:
            copies = send_field(rv.at[m], 2 * m + 2)
            span_copies = send_span(rv.at[m], m + 1)
            unsent += [c.wait_send for c in (*copies.values(), *span_copies)]
        unsent += [c.wait_send for c in slope_copies.values()]
        rr = product(r, r)
        q = r

    value = local_sums({22: rr})
    for stage in range(3):
        sum_start(abuf.at[STEPS], a_send.at[STEPS], a_recv.at[STEPS], stage, value)
        value = sum_finish(abuf.at[STEPS], a_recv.at[STEPS], stage)
    beta = jnp.sqrt(value[:, 22:23] / count + EPSILON)
    scale = 1.0 / beta
    nvs[STEPS - 1] = jnp.concatenate([x * scale for x in q], axis=0)
    pltpu.make_async_copy(nvs.at[STEPS - 1], nv_any.at[STEPS - 1], out_sem.at[STEPS - 1]).start()
    hess[-1] = jnp.where(iota((1, CAP), 1) == 22, beta, hess[-1])
    hess_ref[...] = jnp.concatenate(hess, axis=0)[:, 0:23]

    for c in (*first.values(), *first_span, *messages.values()):
        c.wait_send()
    for c in unsent:
        if callable(c):
            c()
        else:
            c.wait()
    for m in range(STEPS):
        pltpu.make_async_copy(nvs.at[m], nv_any.at[m], out_sem.at[m]).wait()


def on_device(grid, krylov, limiter, pseudo_diag, face_states, face_angle, face_area, slope_weight,
              span_coupling, face_cells, send_list, send_count):
    ns, ny, nz = grid
    count = float(5 * 4 * CELLS * ns * ny * nz)

    def halves(x):
        lead = x.shape[:-2]
        x = x.reshape(*lead, 4, 2, CAP)
        return jnp.swapaxes(x, -3, -2).reshape(*lead, 8, CAP)

    pack = jnp.stack(
        [
            face_angle,
            face_area,
            slope_weight,
            face_cells[0].astype(F32),
            face_cells[1].astype(F32),
            jnp.pad(span_coupling, (0, FACES - CELLS)),
            jnp.zeros((FACES,), F32),
            jnp.zeros((FACES,), F32),
        ]
    )
    anywhere = pl.BlockSpec(memory_space=pl.ANY)
    members = ns + ny + nz
    dma = pltpu.SemaphoreType.DMA
    vectors, hess = pl.pallas_call(
        functools.partial(kernel, grid, count),
        out_shape=(
            jax.ShapeDtypeStruct((STEPS, 40, CAP), F32),
            jax.ShapeDtypeStruct((STEPS, 23), F32),
        ),
        in_specs=[anywhere] * 6,
        out_specs=(anywhere, pl.BlockSpec(memory_space=pltpu.VMEM)),
        scratch_shapes=[
            pltpu.VMEM((NVEC * 40, CAP), F32),
            pltpu.VMEM((5, 8, CAP), F32),
            pltpu.VMEM((8, CAP), F32),
            pltpu.VMEM((2, 5, 4, FACES), F32),
            pltpu.VMEM((8, FACES), F32),
            pltpu.VMEM((4, CAP), jnp.int32),
            pltpu.VMEM((STEPS, 40, CAP), F32),
            pltpu.VMEM((STEPS, 40, CAP), F32),
            pltpu.VMEM((STEPS, 40, CAP), F32),
            pltpu.VMEM((CELLS, 1536), BF16),
            pltpu.VMEM((CELLS, 2048), BF16),
            pltpu.VMEM((4, CELLS, 2 * CAP), BF16),
            pltpu.VMEM((5, 8, FACES), F32),
            pltpu.VMEM((5, 8, FACES), F32),
            pltpu.VMEM((8, FACES), F32),
            pltpu.VMEM((2, 8, FACES), F32),
            pltpu.VMEM((4, 48, CAP), F32),
            pltpu.VMEM((4, 48, CAP), F32),
            pltpu.VMEM((2 * STEPS, 4, 40, CAP), F32),
            pltpu.VMEM((STEPS, 2, 40, CAP), F32),
            pltpu.VMEM((members, 8, CAP), F32),
            pltpu.VMEM((STEPS + 1, members, 1, CAP), F32),
            dma((6,)),
            dma((STEPS,)),
            dma((4,)),
            dma((4,)),
            dma((2 * STEPS, 4)),
            dma((2 * STEPS, 4)),
            dma((STEPS, 2)),
            dma((STEPS, 2)),
            dma((3,)),
            dma((3,)),
            dma((STEPS + 1, 3)),
            dma((STEPS + 1, 3)),
        ],
        compiler_params=pltpu.CompilerParams(
            collective_id=0, has_side_effects=True, vmem_limit_bytes=48 * 2**20
        ),
    )(halves(krylov).reshape(NVEC * 40, CAP), halves(limiter), halves(pseudo_diag), face_states, pack, send_list)
    vectors = jnp.swapaxes(vectors.reshape(STEPS, 5, 2, 4, CAP), 2, 3)
    return vectors.reshape(STEPS, 5, 4, CELLS), hess


def solution(mesh):
    ns, nd = mesh.shape["span"], mesh.shape["dom"]
    ny = 4 if nd >= 16 else 2
    return jax.shard_map(
        functools.partial(on_device, (ns, ny, nd // ny)),
        mesh=mesh,
        in_specs=(
            P(None, None, "span", "dom"),
            P(None, "span", "dom"),
            P("span", "dom"),
            P(None, None, "span", "dom"),
            P("dom"),
            P("dom"),
            P("dom"),
            P("dom"),
            P(None, "dom"),
            P(None, "dom"),
            P(None, "dom"),
        ),
        out_specs=(P(None, None, "span", "dom"), P()),
        check_vma=False,
    )
```

```python
import functools

import jax
import jax.numpy as jnp
from jax import lax
from jax.experimental import pallas as pl
from jax.experimental.pallas import tpu as pltpu
from jax.sharding import PartitionSpec as P

MESH = pl.DeviceIdType.MESH
OFFSETS = (-2, -1, 1, 2)
NEAR = (1, 2, 0, 3)
EPSILON = 1e-06
F32 = jnp.float32
BF16 = jnp.bfloat16
STEPS = 3
NVEC = 20
CELLS = 256
FACES = 512
CAP = 128


def dot_nn(a, b):
    return lax.dot_general(a, b, (((1,), (0,)), ((), ())), preferred_element_type=F32)


def dot_nt(a, b):
    return lax.dot_general(a, b, (((1,), (1,)), ((), ())), preferred_element_type=F32)


def iota(shape, dim):
    return lax.broadcasted_iota(jnp.int32, shape, dim)


def top_rows(shape):
    return (iota(shape, 0) & 4) == 0


def flip(x):
    return pltpu.roll(x, 4, 0)


def split2(x):
    hi = x.astype(BF16).astype(F32)
    return jnp.concatenate([hi, x - hi], axis=0)


def split3(x):
    hi = x.astype(BF16).astype(F32)
    rest = x - hi
    mid = rest.astype(BF16).astype(F32)
    return jnp.concatenate([hi, mid, rest - mid], axis=0)


def operand(fields):
    both = split2(jnp.concatenate(fields, axis=0))
    top = top_rows(both.shape)
    return jnp.concatenate([jnp.where(top, both, 0.0), jnp.where(top, 0.0, both)], axis=1).astype(BF16)


def joined(y):
    half = y.shape[0] // 2
    return y[:half] + y[half:]


def packed_cells(y):
    out = []
    for v in range(5):
        low, high = y[8 * v : 8 * v + 8, :CAP], y[8 * v : 8 * v + 8, CAP:]
        top = top_rows(low.shape)
        out.append(jnp.where(top, low, high) + flip(jnp.where(top, high, low)))
    return out


def one_hot(size, row):
    return (iota((size, row.shape[1]), 0) == row).astype(F32)


def kernel(
    grid,
    count,
    k_any,
    lim_any,
    pd_any,
    fs_any,
    angle_any,
    area_any,
    weight_any,
    coupling_any,
    cells_any,
    sl_any,
    nv_any,
    hess_ref,
    kv,
    limv,
    pdv,
    fsv,
    anglev,
    areav,
    weightv,
    couplingv,
    cellsv,
    slv,
    nvs,
    sv,
    rv,
    w_own,
    w_sc,
    w_nb,
    cf_int,
    cf_gf,
    pl_int,
    pl_gf,
    msg_out,
    msg_in,
    nbuf,
    sbuf,
    gbuf,
    abuf,
    load_sem,
    out_sem,
    msg_send,
    msg_recv,
    nb_send,
    nb_recv,
    sp_send,
    sp_recv,
    g_send,
    g_recv,
    a_send,
    a_recv,
):
    ns, ny, nz = grid
    nd = ny * nz
    s = lax.axis_index("span")
    d = lax.axis_index("dom")
    y, z = d // nz, lax.rem(d, nz)

    def dom_at(offset):
        return lax.rem(d + (offset + nd), nd)

    def span_at(offset):
        return lax.rem(s + (offset + ns), ns)

    xs = ns // 2
    x, core = s // 2, lax.rem(s, 2)
    places = (s * ny + y, z)
    sizes = (ns * ny, nz)
    starts = (0, ns * ny)

    def others(stage):
        if stage:
            hops = sorted(range(1, nz), key=lambda k: -min(k, nz - k))
            return [(s, y * nz + lax.rem(z + k, nz)) for k in hops]
        hops = [(i, c, k) for i in range(xs) for c in range(2) for k in range(ny)]
        hops = sorted(hops, key=lambda h: -(min(h[0], xs - h[0]) + min(h[2], ny - h[2])))
        return [
            (lax.rem(x + i, xs) * 2 + lax.rem(core + c, 2), lax.rem(y + k, ny) * nz + z)
            for i, c, k in hops
            if (i, c, k) != (0, 0, 0)
        ]

    barrier = pltpu.get_barrier_semaphore()
    partners = [(s, dom_at(o)) for o in OFFSETS] + others(0) + others(1)
    for device in partners:
        pl.semaphore_signal(barrier, inc=1, device_id=device, device_id_type=MESH)

    pairs = (
        (fs_any, fsv),
        (angle_any, anglev),
        (area_any, areav),
        (weight_any, weightv),
        (cells_any, cellsv),
        (sl_any, slv),
        (k_any, kv),
        (coupling_any, couplingv),
        (lim_any, limv),
        (pd_any, pdv),
    )
    loads = [pltpu.make_async_copy(src, dst, load_sem.at[i]) for i, (src, dst) in enumerate(pairs)]
    for load in loads:
        load.start()

    exists = [(d + o >= 0) & (d + o < nd) for o in OFFSETS]
    for j in range(4):

        @pl.when(jnp.logical_not(exists[j]))
        def _():
            msg_in[j] = jnp.zeros((48, CAP), F32)
            for number in range(2 * STEPS):
                nbuf[number, j] = jnp.zeros((40, CAP), F32)

    def when(condition, action):
        @pl.when(condition)
        def _():
            action()

    def send_field(src, number):
        copies = []
        for j in NEAR:
            copy = pltpu.make_async_remote_copy(
                src_ref=src,
                dst_ref=nbuf.at[number, 3 - j],
                send_sem=nb_send.at[number, j],
                recv_sem=nb_recv.at[number, 3 - j],
                device_id=(s, dom_at(OFFSETS[j])),
                device_id_type=MESH,
            )
            when(exists[j], copy.start)
            copies.append((j, copy))
        return dict(copies)

    def send_span(src, number):
        copies = []
        for side, offset in ((0, 1), (1, -1)):
            copy = pltpu.make_async_remote_copy(
                src_ref=src,
                dst_ref=sbuf.at[number, side],
                send_sem=sp_send.at[number, side],
                recv_sem=sp_recv.at[number, side],
                device_id=(span_at(offset), d),
                device_id_type=MESH,
            )
            copy.start()
            copies.append(copy)
        return copies

    unsent = []

    def sum_start(buf, send, recv, stage, value):
        place = buf.at[starts[stage] + places[stage]]
        buf[pl.ds(starts[stage] + places[stage], 1)] = value[None]
        for device in others(stage):
            pltpu.make_async_remote_copy(
                src_ref=place,
                dst_ref=place,
                send_sem=send.at[stage],
                recv_sem=recv.at[stage],
                device_id=device,
                device_id_type=MESH,
            ).start()
        span = buf.at[pl.ds(starts[stage], sizes[stage] - 1)]
        unsent.append(pltpu.make_async_copy(span, span, send.at[stage]).wait)

    def sum_finish(buf, recv, stage):
        n = sizes[stage]
        span = buf.at[pl.ds(starts[stage], n - 1)]
        pltpu.make_async_copy(span, span, recv.at[stage]).wait()
        terms = [buf[starts[stage] + k] for k in range(n)]
        while len(terms) > 1:
            terms = [sum(terms[i + 1 : i + 2], terms[i]) for i in range(0, len(terms), 2)]
        return terms[0]

    for load in loads[:5]:
        load.wait()
    angle, area, weight = anglev[...], areav[...], weightv[...]
    owner, other = cellsv[0:1, :], cellsv[1:2, :]
    nx, ny_ = jnp.cos(angle), jnp.sin(angle)
    state = [jnp.concatenate([fsv[0, v], fsv[1, v]], axis=0) for v in range(5)]
    inv = 1.0 / state[0]
    u1, u2, u3 = state[1] * inv, state[2] * inv, state[3] * inv
    pressure = 0.4 * (state[4] - 0.5 * (state[1] * u1 + state[2] * u2 + state[3] * u3))
    enthalpy = (state[4] + pressure) * inv
    speed = jnp.abs(u1 * nx + u2 * ny_) + jnp.sqrt(1.4 * pressure * inv)
    lam = jnp.maximum(speed, flip(speed))
    lam = jnp.where(top_rows(lam.shape), lam, -lam)
    half_area = 0.5 * area
    coefs = [u1, u2, u3, enthalpy, lam]
    for i, c in enumerate(coefs):
        cf_int[i] = c
    inside = (other < CELLS).astype(F32)
    pl_int[0:1, :] = nx
    pl_int[1:2, :] = ny_
    pl_int[2:3, :] = half_area * inside
    pl_int[3:4, :] = weight * inside
    pl_int[4:8, :] = jnp.zeros((4, FACES), F32)

    loads[5].wait()
    plane_rows = jnp.concatenate(
        [nx, ny_, half_area, weight, owner.astype(F32), jnp.zeros((3, FACES), F32)], axis=0
    )
    gathered = split3(jnp.concatenate([*coefs, plane_rows], axis=0)).astype(BF16)
    for j in range(4):
        slots = (iota((CAP, FACES), 0) + (CELLS + j * CAP) == other).astype(F32).astype(BF16)
        part = dot_nt(gathered, slots)
        part = part[0:48] + part[48:96] + part[96:144]
        msg_out[j, 0:45, :] = part[0:45]
        msg_out[j, 45:46, :] = slv[3 - j : 4 - j, :].astype(F32)
        msg_out[j, 46:48, :] = jnp.zeros((2, CAP), F32)

    pl.semaphore_wait(barrier, len(partners))

    first = send_field(k_any.at[pl.ds(40 * NVEC - 40, 40)], 0)
    messages = {}
    for j in NEAR:
        copy = pltpu.make_async_remote_copy(
            src_ref=msg_out.at[j],
            dst_ref=msg_in.at[j],
            send_sem=msg_send.at[j],
            recv_sem=msg_recv.at[j],
            device_id=(s, dom_at(OFFSETS[3 - j])),
            device_id_type=MESH,
        )
        when(exists[3 - j], copy.start)
        messages[j] = copy
    first_span = send_span(k_any.at[pl.ds(40 * NVEC - 40, 40)], 0)

    loads[6].wait()
    total = jnp.zeros((72, 72), F32)
    for pair in range(20):
        rows = jnp.concatenate(
            [kv[pl.ds(2 * pair + i, NVEC, stride=40), :] for i in range(2)], axis=1
        )
        rows = jnp.concatenate([rows, jnp.zeros((4, 2 * CAP), F32)], axis=0)
        rows = split3(rows).astype(BF16)
        total = total + dot_nt(rows, rows)
    rows = total[0:24] + total[24:48] + total[48:72]
    gram = rows[:, 0:24] + rows[:, 24:48] + rows[:, 48:72]
    gram = jnp.concatenate([gram, jnp.zeros((24, CAP - 24), F32)], axis=1)
    gram = gram[0:8] + pltpu.roll(gram[8:16], 32, 1) + pltpu.roll(gram[16:24], 64, 1)
    sum_start(gbuf, g_send, g_recv, 0, gram)

    hot_a, hot_b = one_hot(CELLS, owner), one_hot(CELLS, other)
    w_own[:, 0:512] = (hot_a - hot_b).astype(BF16)
    w_sc[:, 0:512] = hot_a.astype(BF16)
    w_sc[:, 512:1024] = hot_b.astype(BF16)
    for j in range(4):
        at = 512 + j * CAP
        hot = one_hot(CELLS, msg_out[j, 44:45, :].astype(jnp.int32)).astype(BF16)
        w_own[:, at : at + CAP] = hot
        w_sc[:, at + 512 : at + 512 + CAP] = hot
        hot = one_hot(CELLS, slv[j : j + 1, :])
        w_own[:, at + 512 : at + 512 + CAP] = (-hot).astype(BF16)
        w_sc[:, at + 1024 : at + 1024 + CAP] = hot.astype(BF16)

    gram = sum_finish(gbuf, g_recv, 0)
    sum_start(gbuf, g_send, g_recv, 1, gram)

    for j in NEAR:
        when(exists[j], messages[j].wait_recv)
        at = j * CAP
        for i in range(5):
            mine, theirs = msg_out[j, 8 * i : 8 * i + 8, :], msg_in[j, 8 * i : 8 * i + 8, :]
            cf_gf[i, :, at : at + CAP] = jnp.where(top_rows(mine.shape), mine, theirs)
        for side, msg in ((0, msg_out), (1, msg_in)):
            pl_gf[side, :, at : at + CAP] = msg[j, 40:48, :]
        w_nb[j, :, 0:CAP] = (-one_hot(CELLS, msg_in[j, 45:46, :].astype(jnp.int32))).astype(BF16)
        w_nb[j, :, CAP:] = one_hot(CELLS, msg_in[j, 44:45, :].astype(jnp.int32)).astype(BF16)

    def jumps(own, number, copies):
        near = joined(dot_nn(operand(own), w_own[...]))
        ghost = [None] * 4
        foreign = [None] * 4
        for j in NEAR:
            when(exists[j], copies[3 - j].wait_recv)
            part = joined(dot_nn(operand([nbuf[number, j]]), w_nb[j]))
            ghost[3 - j] = part[:, :CAP]
            foreign[j] = part[:, CAP:]
        return (
            near[:, 0:512],
            near[:, 512:1024] + jnp.concatenate(ghost, axis=1),
            near[:, 1024:1536] + jnp.concatenate(foreign, axis=1),
        )

    def transposed(e, cf, nx, ny, half_area):
        e = [half_area * x for x in e]
        u1, u2, u3, enthalpy, lam = (cf[i] for i in range(5))
        vn = u1 * nx + u2 * ny
        phi = 0.2 * (u1 * u1 + u2 * u2 + u3 * u3)
        cp = e[1] * nx + e[2] * ny + e[4] * vn
        ch = e[0] + e[1] * u1 + e[2] * u2 + e[3] * u3 + e[4] * enthalpy
        diag = vn + lam
        cp4 = 0.4 * cp
        return [
            e[0] * diag + cp * phi - ch * vn,
            e[1] * diag - u1 * cp4 + ch * nx,
            e[2] * diag - u2 * cp4 + ch * ny,
            e[3] * diag - u3 * cp4,
            e[4] * diag + cp4,
        ]

    def state_part(own, number, copies):
        e_int, e_gh, e_for = jumps(own, number, copies)
        jump_int, jump_gf = [], []
        for v in range(5):
            x = e_int[8 * v : 8 * v + 8]
            jump_int.append(x + flip(x))
            g, f = e_gh[8 * v : 8 * v + 8], e_for[8 * v : 8 * v + 8]
            top = top_rows(g.shape)
            jump_gf.append(jnp.where(top, g, f) + flip(jnp.where(top, f, g)))
        g_int = transposed(jump_int, cf_int, pl_int[0:1, :], pl_int[1:2, :], pl_int[2:3, :])
        top = top_rows((8, FACES))
        rows = [jnp.where(top, pl_gf[0, i : i + 1, :], pl_gf[1, i : i + 1, :]) for i in range(3)]
        g_gf = transposed(jump_gf, cf_gf, *rows)
        parts = []
        for g in (jnp.concatenate(g_int, axis=0), jnp.concatenate(g_gf, axis=0)):
            top = top_rows(g.shape)
            parts += [jnp.where(top, g, 0.0), jnp.where(top, 0.0, g)]
        lhs = split2(jnp.concatenate(parts, axis=1)).astype(BF16)
        return packed_cells(joined(dot_nt(lhs, w_sc[...])))

    def slope_part(own, number, copies):
        d_int, d_gh, d_for = jumps(own, number, copies)
        lhs = jnp.concatenate(
            [d_int * pl_int[3:4, :], d_gh * pl_gf[0, 3:4, :], d_for * pl_gf[1, 3:4, :]], axis=1
        )
        return packed_cells(joined(dot_nt(split2(lhs).astype(BF16), w_own[...])))

    row = iota((8, CAP), 0)
    layer = row & 3
    loads[7].wait()
    coupling = jnp.where(row < 4, couplingv[:, 0:CAP], couplingv[:, CAP:])
    eye = iota((24, CAP), 0) == iota((24, CAP), 1)
    row24 = iota((24, CAP), 0)

    def row_of(column):
        return jnp.sum(jnp.where(eye, column, 0.0), axis=0, keepdims=True)

    def local_sums(terms):
        rows = []
        for i in range(24):
            if i in terms:
                rows.append(jnp.sum(terms[i], axis=0, keepdims=True))
            else:
                rows.append(jnp.zeros((1, CAP), F32))
        return row_of(jnp.sum(jnp.concatenate(rows, axis=0), axis=1, keepdims=True))

    def product(a, b):
        out = a[0] * b[0]
        for v in range(1, 5):
            out = out + a[v] * b[v]
        return out

    def basis(i):
        return [kv[40 * i + 8 * v : 40 * i + 8 * v + 8, :] for v in range(5)]

    q = basis(NVEC - 1)
    copies, span_copies = first, first_span
    inverse = None
    done = []
    rr = None
    hess = []
    norms = []
    for m in range(STEPS):
        state_terms = state_part(q, 2 * m, copies)
        if m == 0:
            loads[8].wait()
            loads[9].wait()
        slope_field = [limv[v] * state_terms[v] for v in range(5)]
        sv[m] = jnp.concatenate(slope_field, axis=0)
        slope_copies = send_field(sv.at[m], 2 * m + 1)
        for copy in span_copies:
            copy.wait_recv()
        local = []
        for v in range(5):
            above = jnp.where(layer == 0, pltpu.roll(sbuf[m, 0, 8 * v : 8 * v + 8, :], 5, 0), pltpu.roll(q[v], 1, 0))
            below = jnp.where(layer == 3, pltpu.roll(sbuf[m, 1, 8 * v : 8 * v + 8, :], 3, 0), pltpu.roll(q[v], 7, 0))
            local.append(
                pdv[...] * q[v] + coupling * (2.0 * q[v] - above - below) + state_terms[v]
            )
        if m == 0:
            gram = sum_finish(gbuf, g_recv, 1) / count
            wide = jnp.concatenate(
                [gram, pltpu.roll(gram, CAP - 32, 1), pltpu.roll(gram, CAP - 64, 1)], axis=0
            )
            lane = iota((24, CAP), 1)
            kept = (lane < NVEC) & (row24 < NVEC)
            diagonal = (row24 == lane) & (row24 >= NVEC)
            gram_mean = jnp.where(kept, wide, 0.0)
            work = gram_mean + jnp.where(diagonal | (lane == row24 + 32), 1.0, 0.0)
            for k in range(NVEC):
                column = jnp.sum(jnp.where(lane == k, work, 0.0), axis=1, keepdims=True)
                pivot = work[k : k + 1, :]
                scale = 1.0 / column[k : k + 1, :]
                work = work - (column - jnp.where(row24[:, 0:1] == k, 1.0, 0.0)) * (pivot * scale)
            inverse = pltpu.roll(work, CAP - 32, 1)
        slope_terms = slope_part(slope_field, 2 * m + 1, slope_copies)
        w = [local[v] - slope_terms[v] for v in range(5)]

        terms = {i: product(basis(i), w) for i in range(NVEC)}
        for i, vector in enumerate(done):
            terms[NVEC + i] = product(vector, w)
        if m:
            terms[NVEC + m - 1] = product(q, w)
            terms[22] = rr
        if m == STEPS - 1:
            terms[23] = product(w, w)
        value = local_sums(terms)
        for stage in range(2):
            sum_start(abuf.at[m], a_send.at[m], a_recv.at[m], stage, value)
            value = sum_finish(abuf.at[m], a_recv.at[m], stage)
        value = value / count
        solved = jnp.sum(inverse * value, axis=1, keepdims=True)
        if m:
            norms.append(solved[22:23, :])
            ww = solved[23:24, :]
            beta = jnp.sqrt(norms[-1] + EPSILON)
            scale = 1.0 / beta
            last = [x * scale for x in q]
            nvs[m - 1] = jnp.concatenate(last, axis=0)
            pltpu.make_async_copy(nvs.at[m - 1], nv_any.at[m - 1], out_sem.at[m - 1]).start()
            done.append(last)
            hess[-1] = jnp.where(iota((1, CAP), 1) == 22, beta, hess[-1])
            w = [x * scale for x in w]
            solved = solved * scale
            solved = jnp.where(row24[:, 0:1] == NVEC + m - 1, solved * scale, solved)
            if m == 1:
                across = solved[20:21, :]
        hess.append(jnp.where(iota((1, CAP), 1) < NVEC + m, row_of(solved), 0.0))
        wide = jnp.broadcast_to(solved, (24, CAP))
        r = w
        for i in range(NVEC + m):
            c = wide[i : i + 1, :]
            vector = basis(i) if i < NVEC else done[i - NVEC]
            r = [r[v] - c * vector[v] for v in range(5)]
        rv[m] = jnp.concatenate(r, axis=0)
        unsent += [functools.partial(when, exists[j], c.wait_send) for j, c in slope_copies.items()]
        if m + 1 < STEPS:
            copies = send_field(rv.at[m], 2 * m + 2)
            span_copies = send_span(rv.at[m], m + 1)
            unsent += [functools.partial(when, exists[j], c.wait_send) for j, c in copies.items()]
            unsent += [c.wait_send for c in span_copies]
            rr = product(r, r)
        q = r

    n0, n1 = (n / (n + EPSILON) for n in norms)
    cross = across * (1.0 - n0) / jnp.sqrt(norms[1] + EPSILON)
    lane = iota((24, CAP), 1)
    whole = gram_mean + jnp.where((row24 == 20) & (lane == 20), n0, 0.0)
    whole = whole + jnp.where((row24 == 21) & (lane == 21), n1, 0.0)
    whole = whole + jnp.where((row24 + lane == 41) & (row24 >= 20) & (lane >= 20), cross, 0.0)
    c_row = row_of(jnp.where(row24[:, 0:1] < 22, solved, 0.0))
    p_row = value * scale
    p_row = jnp.where(iota((1, CAP), 1) == 21, p_row * scale, p_row)
    inner = jnp.sum(whole * c_row - jnp.where(eye, 2.0 * p_row, 0.0), axis=1, keepdims=True)
    inner = jnp.where(row24[:, 0:1] < 22, inner * solved, 0.0)
    rr = ww * scale * scale + jnp.sum(inner, axis=0, keepdims=True)
    beta = jnp.sqrt(jnp.maximum(rr, 0.0) + EPSILON)
    scale = 1.0 / beta
    nvs[STEPS - 1] = jnp.concatenate([x * scale for x in q], axis=0)
    pltpu.make_async_copy(nvs.at[STEPS - 1], nv_any.at[STEPS - 1], out_sem.at[STEPS - 1]).start()
    hess[-1] = jnp.where(iota((1, CAP), 1) == 22, beta, hess[-1])
    hess_ref[...] = jnp.concatenate(hess, axis=0)[:, 0:23]

    for j in range(4):
        when(exists[j], first[j].wait_send)
        when(exists[3 - j], messages[j].wait_send)
    for c in first_span:
        c.wait_send()
    for wait in unsent:
        wait()
    for m in range(STEPS):
        pltpu.make_async_copy(nvs.at[m], nv_any.at[m], out_sem.at[m]).wait()


def on_device(grid, krylov, limiter, pseudo_diag, face_states, face_angle, face_area, slope_weight,
              span_coupling, face_cells, send_list, send_count):
    ns, ny, nz = grid
    count = float(5 * 4 * CELLS * ns * ny * nz)

    def halves(x):
        lead = x.shape[:-2]
        x = x.reshape(*lead, 4, 2, CAP)
        return jnp.swapaxes(x, -3, -2).reshape(*lead, 8, CAP)

    anywhere = pl.BlockSpec(memory_space=pl.ANY)
    members = ns * ny + nz
    dma = pltpu.SemaphoreType.DMA
    vectors, hess = pl.pallas_call(
        functools.partial(kernel, grid, count),
        out_shape=(
            jax.ShapeDtypeStruct((STEPS, 40, CAP), F32),
            jax.ShapeDtypeStruct((STEPS, 23), F32),
        ),
        in_specs=[anywhere] * 10,
        out_specs=(anywhere, pl.BlockSpec(memory_space=pltpu.VMEM)),
        scratch_shapes=[
            pltpu.VMEM((NVEC * 40, CAP), F32),
            pltpu.VMEM((5, 8, CAP), F32),
            pltpu.VMEM((8, CAP), F32),
            pltpu.VMEM((2, 5, 4, FACES), F32),
            pltpu.VMEM((1, FACES), F32),
            pltpu.VMEM((1, FACES), F32),
            pltpu.VMEM((1, FACES), F32),
            pltpu.VMEM((1, CELLS), F32),
            pltpu.VMEM((2, FACES), jnp.int32),
            pltpu.VMEM((4, CAP), jnp.int32),
            pltpu.VMEM((STEPS, 40, CAP), F32),
            pltpu.VMEM((STEPS, 40, CAP), F32),
            pltpu.VMEM((STEPS, 40, CAP), F32),
            pltpu.VMEM((CELLS, 1536), BF16),
            pltpu.VMEM((CELLS, 2048), BF16),
            pltpu.VMEM((4, CELLS, 2 * CAP), BF16),
            pltpu.VMEM((5, 8, FACES), F32),
            pltpu.VMEM((5, 8, FACES), F32),
            pltpu.VMEM((8, FACES), F32),
            pltpu.VMEM((2, 8, FACES), F32),
            pltpu.VMEM((4, 48, CAP), F32),
            pltpu.VMEM((4, 48, CAP), F32),
            pltpu.VMEM((2 * STEPS, 4, 40, CAP), F32),
            pltpu.VMEM((STEPS, 2, 40, CAP), F32),
            pltpu.VMEM((members, 8, CAP), F32),
            pltpu.VMEM((STEPS, members, 1, CAP), F32),
            dma((10,)),
            dma((STEPS,)),
            dma((4,)),
            dma((4,)),
            dma((2 * STEPS, 4)),
            dma((2 * STEPS, 4)),
            dma((STEPS, 2)),
            dma((STEPS, 2)),
            dma((2,)),
            dma((2,)),
            dma((STEPS, 2)),
            dma((STEPS, 2)),
        ],
        compiler_params=pltpu.CompilerParams(
            collective_id=0, has_side_effects=True, vmem_limit_bytes=60 * 2**20
        ),
    )(
        halves(krylov).reshape(NVEC * 40, CAP),
        halves(limiter),
        halves(pseudo_diag),
        face_states,
        face_angle[None],
        face_area[None],
        slope_weight[None],
        span_coupling[None],
        face_cells,
        send_list,
    )
    vectors = jnp.swapaxes(vectors.reshape(STEPS, 5, 2, 4, CAP), 2, 3)
    return vectors.reshape(STEPS, 5, 4, CELLS), hess


def solution(mesh):
    ns, nd = mesh.shape["span"], mesh.shape["dom"]
    ny = 4 if nd >= 16 else 2
    return jax.shard_map(
        functools.partial(on_device, (ns, ny, nd // ny)),
        mesh=mesh,
        in_specs=(
            P(None, None, "span", "dom"),
            P(None, "span", "dom"),
            P("span", "dom"),
            P(None, None, "span", "dom"),
            P("dom"),
            P("dom"),
            P("dom"),
            P("dom"),
            P(None, "dom"),
            P(None, "dom"),
            P(None, "dom"),
        ),
        out_specs=(P(None, None, "span", "dom"), P()),
        check_vma=False,
    )
```

```python
import functools

import jax
import jax.numpy as jnp
from jax import lax
from jax.experimental import pallas as pl
from jax.experimental.pallas import tpu as pltpu
from jax.sharding import PartitionSpec as P

MESH = pl.DeviceIdType.MESH
OFFSETS = (-2, -1, 1, 2)
NEAR = (1, 2, 0, 3)
EPSILON = 1e-06
F32 = jnp.float32
BF16 = jnp.bfloat16
STEPS = 3
NVEC = 20
CELLS = 256
FACES = 512
CAP = 128


def dot_nn(a, b):
    return lax.dot_general(a, b, (((1,), (0,)), ((), ())), preferred_element_type=F32)


def dot_nt(a, b):
    return lax.dot_general(a, b, (((1,), (1,)), ((), ())), preferred_element_type=F32)


def iota(shape, dim):
    return lax.broadcasted_iota(jnp.int32, shape, dim)


def top_rows(shape):
    return (iota(shape, 0) & 4) == 0


def flip(x):
    return pltpu.roll(x, 4, 0)


def split2(x):
    hi = x.astype(BF16).astype(F32)
    return jnp.concatenate([hi, x - hi], axis=0)


def split3(x):
    hi = x.astype(BF16).astype(F32)
    rest = x - hi
    mid = rest.astype(BF16).astype(F32)
    return jnp.concatenate([hi, mid, rest - mid], axis=0)


def operand(fields):
    both = split2(jnp.concatenate(fields, axis=0))
    top = top_rows(both.shape)
    return jnp.concatenate([jnp.where(top, both, 0.0), jnp.where(top, 0.0, both)], axis=1).astype(BF16)


def joined(y):
    half = y.shape[0] // 2
    return y[:half] + y[half:]


def packed_cells(y):
    out = []
    for v in range(5):
        low, high = y[8 * v : 8 * v + 8, :CAP], y[8 * v : 8 * v + 8, CAP:]
        top = top_rows(low.shape)
        out.append(jnp.where(top, low, high) + flip(jnp.where(top, high, low)))
    return out


def one_hot(size, row):
    return (iota((size, row.shape[1]), 0) == row).astype(F32)


def kernel(
    grid,
    count,
    k_any,
    lim_any,
    pd_any,
    fs_any,
    angle_any,
    area_any,
    weight_any,
    coupling_any,
    cells_any,
    sl_any,
    nv_ref,
    hess_ref,
    kv,
    limv,
    pdv,
    fsv,
    anglev,
    areav,
    weightv,
    couplingv,
    cellsv,
    slv,
    m_slope,
    sv,
    rv,
    w_own,
    w_sc,
    w_nb,
    cf_int,
    cf_gf,
    pl_int,
    pl_gf,
    msg_out,
    msg_in,
    nbuf,
    sbuf,
    gbuf,
    abuf,
    load_sem,
    msg_send,
    msg_recv,
    nb_send,
    nb_recv,
    sp_send,
    sp_recv,
    g_send,
    g_recv,
    a_send,
    a_recv,
):
    ns, ny, nz = grid
    nd = ny * nz
    s = lax.axis_index("span")
    d = lax.axis_index("dom")
    y, z = d // nz, lax.rem(d, nz)

    def dom_at(offset):
        return lax.rem(d + (offset + nd), nd)

    def span_at(offset):
        return lax.rem(s + (offset + ns), ns)

    xs = ns // 2
    x, core = s // 2, lax.rem(s, 2)
    places = (s * ny + y, z)
    sizes = (ns * ny, nz)
    starts = (0, ns * ny)

    def others(stage):
        if stage:
            hops = sorted(range(1, nz), key=lambda k: -min(k, nz - k))
            return [(s, y * nz + lax.rem(z + k, nz)) for k in hops]
        hops = [(i, c, k) for i in range(xs) for c in range(2) for k in range(ny)]
        hops = sorted(hops, key=lambda h: -(min(h[0], xs - h[0]) + min(h[2], ny - h[2])))
        return [
            (lax.rem(x + i, xs) * 2 + lax.rem(core + c, 2), lax.rem(y + k, ny) * nz + z)
            for i, c, k in hops
            if (i, c, k) != (0, 0, 0)
        ]

    barrier = pltpu.get_barrier_semaphore()
    partners = [(s, dom_at(o)) for o in OFFSETS] + others(0) + others(1)
    for device in partners:
        pl.semaphore_signal(barrier, inc=1, device_id=device, device_id_type=MESH)

    pairs = (
        (fs_any, fsv),
        (angle_any, anglev),
        (area_any, areav),
        (weight_any, weightv),
        (cells_any, cellsv),
        (sl_any, slv),
        (k_any, kv),
        (coupling_any, couplingv),
        (lim_any, limv),
        (pd_any, pdv),
    )
    loads = [pltpu.make_async_copy(src, dst, load_sem.at[i]) for i, (src, dst) in enumerate(pairs)]
    for load in loads:
        load.start()

    exists = [(d + o >= 0) & (d + o < nd) for o in OFFSETS]
    for j in range(4):

        @pl.when(jnp.logical_not(exists[j]))
        def _():
            msg_in[j] = jnp.zeros((48, CAP), F32)
            for number in range(2 * STEPS):
                nbuf[number, j] = jnp.zeros((40, CAP), F32)

    def when(condition, action):
        @pl.when(condition)
        def _():
            action()

    def send_field(src, number):
        copies = []
        for j in NEAR:
            copy = pltpu.make_async_remote_copy(
                src_ref=src,
                dst_ref=nbuf.at[number, 3 - j],
                send_sem=nb_send.at[number, j],
                recv_sem=nb_recv.at[number, 3 - j],
                device_id=(s, dom_at(OFFSETS[j])),
                device_id_type=MESH,
            )
            when(exists[j], copy.start)
            copies.append((j, copy))
        return dict(copies)

    def send_span(src, number):
        copies = []
        for side, offset in ((0, 1), (1, -1)):
            copy = pltpu.make_async_remote_copy(
                src_ref=src,
                dst_ref=sbuf.at[number, side],
                send_sem=sp_send.at[number, side],
                recv_sem=sp_recv.at[number, side],
                device_id=(span_at(offset), d),
                device_id_type=MESH,
            )
            copy.start()
            copies.append(copy)
        return copies

    unsent = []

    def sum_start(buf, send, recv, stage, value):
        place = buf.at[starts[stage] + places[stage]]
        buf[pl.ds(starts[stage] + places[stage], 1)] = value[None]
        for device in others(stage):
            pltpu.make_async_remote_copy(
                src_ref=place,
                dst_ref=place,
                send_sem=send.at[stage],
                recv_sem=recv.at[stage],
                device_id=device,
                device_id_type=MESH,
            ).start()
        span = buf.at[pl.ds(starts[stage], sizes[stage] - 1)]
        unsent.append(pltpu.make_async_copy(span, span, send.at[stage]).wait)

    def sum_finish(buf, recv, stage):
        n = sizes[stage]
        span = buf.at[pl.ds(starts[stage], n - 1)]
        pltpu.make_async_copy(span, span, recv.at[stage]).wait()
        terms = [buf[starts[stage] + k] for k in range(n)]
        while len(terms) > 1:
            terms = [sum(terms[i + 1 : i + 2], terms[i]) for i in range(0, len(terms), 2)]
        return terms[0]

    for load in loads[:5]:
        load.wait()
    angle, area, weight = anglev[...], areav[...], weightv[...]
    owner, other = cellsv[0:1, :], cellsv[1:2, :]
    nx, ny_ = jnp.cos(angle), jnp.sin(angle)
    state = [jnp.concatenate([fsv[0, v], fsv[1, v]], axis=0) for v in range(5)]
    inv = 1.0 / state[0]
    u1, u2, u3 = state[1] * inv, state[2] * inv, state[3] * inv
    pressure = 0.4 * (state[4] - 0.5 * (state[1] * u1 + state[2] * u2 + state[3] * u3))
    enthalpy = (state[4] + pressure) * inv
    speed = jnp.abs(u1 * nx + u2 * ny_) + jnp.sqrt(1.4 * pressure * inv)
    lam = jnp.maximum(speed, flip(speed))
    lam = jnp.where(top_rows(lam.shape), lam, -lam)
    half_area = 0.5 * area
    coefs = [u1, u2, u3, enthalpy, lam]
    for i, c in enumerate(coefs):
        cf_int[i] = c
    inside = (other < CELLS).astype(F32)
    pl_int[0:1, :] = nx
    pl_int[1:2, :] = ny_
    pl_int[2:3, :] = half_area * inside
    pl_int[3:4, :] = weight * inside
    pl_int[4:8, :] = jnp.zeros((4, FACES), F32)

    loads[5].wait()
    plane_rows = jnp.concatenate(
        [nx, ny_, half_area, weight, owner.astype(F32), jnp.zeros((3, FACES), F32)], axis=0
    )
    gathered = split3(jnp.concatenate([*coefs, plane_rows], axis=0)).astype(BF16)
    for j in range(4):
        slots = (iota((CAP, FACES), 0) + (CELLS + j * CAP) == other).astype(F32).astype(BF16)
        part = dot_nt(gathered, slots)
        part = part[0:48] + part[48:96] + part[96:144]
        msg_out[j, 0:45, :] = part[0:45]
        msg_out[j, 45:46, :] = slv[3 - j : 4 - j, :].astype(F32)
        msg_out[j, 46:48, :] = jnp.zeros((2, CAP), F32)

    pl.semaphore_wait(barrier, len(partners))

    first = send_field(k_any.at[pl.ds(40 * NVEC - 40, 40)], 0)
    messages = {}
    for j in NEAR:
        copy = pltpu.make_async_remote_copy(
            src_ref=msg_out.at[j],
            dst_ref=msg_in.at[j],
            send_sem=msg_send.at[j],
            recv_sem=msg_recv.at[j],
            device_id=(s, dom_at(OFFSETS[3 - j])),
            device_id_type=MESH,
        )
        when(exists[3 - j], copy.start)
        messages[j] = copy
    first_span = send_span(k_any.at[pl.ds(40 * NVEC - 40, 40)], 0)

    loads[6].wait()
    total = jnp.zeros((72, 72), F32)
    for pair in range(20):
        rows = jnp.concatenate(
            [kv[pl.ds(2 * pair + i, NVEC, stride=40), :] for i in range(2)], axis=1
        )
        rows = jnp.concatenate([rows, jnp.zeros((4, 2 * CAP), F32)], axis=0)
        rows = split3(rows).astype(BF16)
        total = total + dot_nt(rows, rows)
    rows = total[0:24] + total[24:48] + total[48:72]
    gram = rows[:, 0:24] + rows[:, 24:48] + rows[:, 48:72]
    gram = jnp.concatenate([gram, jnp.zeros((24, CAP - 24), F32)], axis=1)
    gram = gram[0:8] + pltpu.roll(gram[8:16], 32, 1) + pltpu.roll(gram[16:24], 64, 1)
    sum_start(gbuf, g_send, g_recv, 0, gram)

    hot_a, hot_b = one_hot(CELLS, owner), one_hot(CELLS, other)
    w_own[:, 0:512] = (hot_a - hot_b).astype(BF16)
    w_sc[:, 0:512] = hot_a.astype(BF16)
    w_sc[:, 512:1024] = hot_b.astype(BF16)
    for j in range(4):
        at = 512 + j * CAP
        hot = one_hot(CELLS, msg_out[j, 44:45, :].astype(jnp.int32)).astype(BF16)
        w_own[:, at : at + CAP] = hot
        w_sc[:, at + 512 : at + 512 + CAP] = hot
        hot = one_hot(CELLS, slv[j : j + 1, :])
        w_own[:, at + 512 : at + 512 + CAP] = (-hot).astype(BF16)
        w_sc[:, at + 1024 : at + 1024 + CAP] = hot.astype(BF16)

    def near(own):
        return joined(dot_nn(operand(own), w_own[...]))

    first_near = near([kv[40 * NVEC - 40 :, :]])

    for j in NEAR:
        when(exists[j], messages[j].wait_recv)
        at = j * CAP
        for i in range(5):
            mine, theirs = msg_out[j, 8 * i : 8 * i + 8, :], msg_in[j, 8 * i : 8 * i + 8, :]
            cf_gf[i, :, at : at + CAP] = jnp.where(top_rows(mine.shape), mine, theirs)
        for side, msg in ((0, msg_out), (1, msg_in)):
            pl_gf[side, :, at : at + CAP] = msg[j, 40:48, :]
        w_nb[j, :, 0:CAP] = (-one_hot(CELLS, msg_in[j, 45:46, :].astype(jnp.int32))).astype(BF16)
        w_nb[j, :, CAP:] = one_hot(CELLS, msg_in[j, 44:45, :].astype(jnp.int32)).astype(BF16)

    def jumps(near, number, copies):
        ghost = [None] * 4
        foreign = [None] * 4
        for j in NEAR:
            when(exists[j], copies[3 - j].wait_recv)
            part = joined(dot_nn(operand([nbuf[number, j]]), w_nb[j]))
            ghost[3 - j] = part[:, :CAP]
            foreign[j] = part[:, CAP:]
        return (
            near[:, 0:512],
            near[:, 512:1024] + jnp.concatenate(ghost, axis=1),
            near[:, 1024:1536] + jnp.concatenate(foreign, axis=1),
        )

    def transposed(e, cf, nx, ny, half_area):
        e = [half_area * x for x in e]
        u1, u2, u3, enthalpy, lam = (cf[i] for i in range(5))
        vn = u1 * nx + u2 * ny
        phi = 0.2 * (u1 * u1 + u2 * u2 + u3 * u3)
        cp = e[1] * nx + e[2] * ny + e[4] * vn
        ch = e[0] + e[1] * u1 + e[2] * u2 + e[3] * u3 + e[4] * enthalpy
        diag = vn + lam
        cp4 = 0.4 * cp
        return [
            e[0] * diag + cp * phi - ch * vn,
            e[1] * diag - u1 * cp4 + ch * nx,
            e[2] * diag - u2 * cp4 + ch * ny,
            e[3] * diag - u3 * cp4,
            e[4] * diag + cp4,
        ]

    def state_part(near, number, copies):
        e_int, e_gh, e_for = jumps(near, number, copies)
        jump_int, jump_gf = [], []
        for v in range(5):
            x = e_int[8 * v : 8 * v + 8]
            jump_int.append(x + flip(x))
            g, f = e_gh[8 * v : 8 * v + 8], e_for[8 * v : 8 * v + 8]
            top = top_rows(g.shape)
            jump_gf.append(jnp.where(top, g, f) + flip(jnp.where(top, f, g)))
        g_int = transposed(jump_int, cf_int, pl_int[0:1, :], pl_int[1:2, :], pl_int[2:3, :])
        top = top_rows((8, FACES))
        rows = [jnp.where(top, pl_gf[0, i : i + 1, :], pl_gf[1, i : i + 1, :]) for i in range(3)]
        g_gf = transposed(jump_gf, cf_gf, *rows)
        parts = []
        for g in (jnp.concatenate(g_int, axis=0), jnp.concatenate(g_gf, axis=0)):
            top = top_rows(g.shape)
            parts += [jnp.where(top, g, 0.0), jnp.where(top, 0.0, g)]
        lhs = split2(jnp.concatenate(parts, axis=1)).astype(BF16)
        return packed_cells(joined(dot_nt(lhs, w_sc[...])))

    def slope_matrices():
        def store(index, faces, weights, cells):
            hi = weights.astype(BF16)
            lo = (weights - hi.astype(F32)).astype(BF16)
            matrix = dot_nt(faces * hi, cells) + dot_nt(faces * lo, cells)
            hi = matrix.astype(BF16)
            m_slope[index, :, 0:CELLS] = hi
            m_slope[index, :, CELLS:] = (matrix - hi.astype(F32)).astype(BF16)

        for j in range(4):
            g, f = (3 - j) * CAP, j * CAP
            weights = jnp.concatenate([pl_gf[0, 3:4, g : g + CAP], pl_gf[1, 3:4, f : f + CAP]], axis=1)
            cells = jnp.concatenate(
                [w_own[:, 512 + g : 512 + g + CAP], w_own[:, 1024 + f : 1024 + f + CAP]], axis=1
            )
            store(j, w_nb[j], weights, cells)
        weights = jnp.concatenate([pl_int[3:4, :], pl_gf[0, 3:4, :], pl_gf[1, 3:4, :]], axis=1)
        store(4, w_own[...], weights, w_own[...])

    def slope_near(own):
        return dot_nn(operand(own), m_slope[4])

    def slope_part(total, number, copies):
        for j in NEAR:
            when(exists[j], copies[3 - j].wait_recv)
            total = total + dot_nn(operand([nbuf[number, j]]), m_slope[j])
        total = joined(total)
        return packed_cells(total[:, :CELLS] + total[:, CELLS:])

    row = iota((8, CAP), 0)
    layer = row & 3
    loads[7].wait()
    coupling = jnp.where(row < 4, couplingv[:, 0:CAP], couplingv[:, CAP:])
    eye = iota((24, CAP), 0) == iota((24, CAP), 1)
    row24 = iota((24, CAP), 0)

    def row_of(column):
        return jnp.sum(jnp.where(eye, column, 0.0), axis=0, keepdims=True)

    def local_sums(terms):
        rows = []
        for i in range(24):
            if i in terms:
                rows.append(jnp.sum(terms[i], axis=0, keepdims=True))
            else:
                rows.append(jnp.zeros((1, CAP), F32))
        return row_of(jnp.sum(jnp.concatenate(rows, axis=0), axis=1, keepdims=True))

    def product(a, b):
        out = a[0] * b[0]
        for v in range(1, 5):
            out = out + a[v] * b[v]
        return out

    def basis(i):
        return [kv[40 * i + 8 * v : 40 * i + 8 * v + 8, :] for v in range(5)]

    q = basis(NVEC - 1)
    copies, span_copies = first, first_span
    inverse = None
    done = []
    rr = None
    hess = []
    norms = []
    for m in range(STEPS):
        state_terms = state_part(near(q) if m else first_near, 2 * m, copies)
        if m == 0:
            loads[8].wait()
            loads[9].wait()
        slope_field = [limv[v] * state_terms[v] for v in range(5)]
        sv[m] = jnp.concatenate(slope_field, axis=0)
        slope_copies = send_field(sv.at[m], 2 * m + 1)
        if m == 0:
            slope_matrices()
            gram = sum_finish(gbuf, g_recv, 0)
            sum_start(gbuf, g_send, g_recv, 1, gram)
        slope_own = slope_near(slope_field)
        for copy in span_copies:
            copy.wait_recv()
        local = []
        for v in range(5):
            above = jnp.where(layer == 0, pltpu.roll(sbuf[m, 0, 8 * v : 8 * v + 8, :], 5, 0), pltpu.roll(q[v], 1, 0))
            below = jnp.where(layer == 3, pltpu.roll(sbuf[m, 1, 8 * v : 8 * v + 8, :], 3, 0), pltpu.roll(q[v], 7, 0))
            local.append(
                pdv[...] * q[v] + coupling * (2.0 * q[v] - above - below) + state_terms[v]
            )
        slope_terms = slope_part(slope_own, 2 * m + 1, slope_copies)
        w = [local[v] - slope_terms[v] for v in range(5)]

        terms = {i: product(basis(i), w) for i in range(NVEC)}
        for i, vector in enumerate(done):
            terms[NVEC + i] = product(vector, w)
        if m:
            terms[NVEC + m - 1] = product(q, w)
            terms[22] = rr
        if m == STEPS - 1:
            terms[23] = product(w, w)
        value = local_sums(terms)
        sum_start(abuf.at[m], a_send.at[m], a_recv.at[m], 0, value)
        if m == 0:
            gram = sum_finish(gbuf, g_recv, 1) / count
            wide = jnp.concatenate(
                [gram, pltpu.roll(gram, CAP - 32, 1), pltpu.roll(gram, CAP - 64, 1)], axis=0
            )
            lane = iota((24, CAP), 1)
            kept = (lane < NVEC) & (row24 < NVEC)
            diagonal = (row24 == lane) & (row24 >= NVEC)
            gram_mean = jnp.where(kept, wide, 0.0)
            work = gram_mean + jnp.where(diagonal | (lane == row24 + 32), 1.0, 0.0)
            for k in range(NVEC):
                column = jnp.sum(jnp.where(lane == k, work, 0.0), axis=1, keepdims=True)
                pivot = work[k : k + 1, :]
                scale = 1.0 / column[k : k + 1, :]
                work = work - (column - jnp.where(row24[:, 0:1] == k, 1.0, 0.0)) * (pivot * scale)
            inverse = pltpu.roll(work, CAP - 32, 1)
        value = sum_finish(abuf.at[m], a_recv.at[m], 0)
        sum_start(abuf.at[m], a_send.at[m], a_recv.at[m], 1, value)
        value = sum_finish(abuf.at[m], a_recv.at[m], 1)
        value = value / count
        solved = jnp.sum(inverse * value, axis=1, keepdims=True)
        if m:
            norms.append(solved[22:23, :])
            ww = solved[23:24, :]
            beta = jnp.sqrt(norms[-1] + EPSILON)
            scale = 1.0 / beta
            last = [x * scale for x in q]
            nv_ref[m - 1] = jnp.concatenate(last, axis=0)
            done.append(last)
            hess[-1] = jnp.where(iota((1, CAP), 1) == 22, beta, hess[-1])
            w = [x * scale for x in w]
            solved = solved * scale
            solved = jnp.where(row24[:, 0:1] == NVEC + m - 1, solved * scale, solved)
            if m == 1:
                across = solved[20:21, :]
        hess.append(jnp.where(iota((1, CAP), 1) < NVEC + m, row_of(solved), 0.0))
        wide = jnp.broadcast_to(solved, (24, CAP))
        r = w
        for i in range(NVEC + m):
            c = wide[i : i + 1, :]
            vector = basis(i) if i < NVEC else done[i - NVEC]
            r = [r[v] - c * vector[v] for v in range(5)]
        rv[m] = jnp.concatenate(r, axis=0)
        unsent += [functools.partial(when, exists[j], c.wait_send) for j, c in slope_copies.items()]
        if m + 1 < STEPS:
            copies = send_field(rv.at[m], 2 * m + 2)
            span_copies = send_span(rv.at[m], m + 1)
            unsent += [functools.partial(when, exists[j], c.wait_send) for j, c in copies.items()]
            unsent += [c.wait_send for c in span_copies]
            rr = product(r, r)
        q = r

    n0, n1 = (n / (n + EPSILON) for n in norms)
    cross = across * (1.0 - n0) / jnp.sqrt(norms[1] + EPSILON)
    lane = iota((24, CAP), 1)
    whole = gram_mean + jnp.where((row24 == 20) & (lane == 20), n0, 0.0)
    whole = whole + jnp.where((row24 == 21) & (lane == 21), n1, 0.0)
    whole = whole + jnp.where((row24 + lane == 41) & (row24 >= 20) & (lane >= 20), cross, 0.0)
    c_row = row_of(jnp.where(row24[:, 0:1] < 22, solved, 0.0))
    p_row = value * scale
    p_row = jnp.where(iota((1, CAP), 1) == 21, p_row * scale, p_row)
    inner = jnp.sum(whole * c_row - jnp.where(eye, 2.0 * p_row, 0.0), axis=1, keepdims=True)
    inner = jnp.where(row24[:, 0:1] < 22, inner * solved, 0.0)
    rr = ww * scale * scale + jnp.sum(inner, axis=0, keepdims=True)
    beta = jnp.sqrt(jnp.maximum(rr, 0.0) + EPSILON)
    scale = 1.0 / beta
    nv_ref[STEPS - 1] = jnp.concatenate([x * scale for x in q], axis=0)
    hess[-1] = jnp.where(iota((1, CAP), 1) == 22, beta, hess[-1])
    hess_ref[...] = jnp.concatenate(hess, axis=0)[:, 0:23]

    for j in range(4):
        when(exists[j], first[j].wait_send)
        when(exists[3 - j], messages[j].wait_send)
    for c in first_span:
        c.wait_send()
    for wait in unsent:
        wait()


def on_device(grid, krylov, limiter, pseudo_diag, face_states, face_angle, face_area, slope_weight,
              span_coupling, face_cells, send_list, send_count):
    ns, ny, nz = grid
    count = float(5 * 4 * CELLS * ns * ny * nz)

    def halves(x):
        lead = x.shape[:-2]
        x = x.reshape(*lead, 4, 2, CAP)
        return jnp.swapaxes(x, -3, -2).reshape(*lead, 8, CAP)

    anywhere = pl.BlockSpec(memory_space=pl.ANY)
    members = ns * ny + nz
    dma = pltpu.SemaphoreType.DMA
    vectors, hess = pl.pallas_call(
        functools.partial(kernel, grid, count),
        out_shape=(
            pltpu.VMEM((STEPS, 40, CAP), F32),
            pltpu.VMEM((STEPS, 23), F32),
        ),
        in_specs=[anywhere] * 10,
        out_specs=(pl.BlockSpec(memory_space=pltpu.VMEM),) * 2,
        scratch_shapes=[
            pltpu.VMEM((NVEC * 40, CAP), F32),
            pltpu.VMEM((5, 8, CAP), F32),
            pltpu.VMEM((8, CAP), F32),
            pltpu.VMEM((2, 5, 4, FACES), F32),
            pltpu.VMEM((1, FACES), F32),
            pltpu.VMEM((1, FACES), F32),
            pltpu.VMEM((1, FACES), F32),
            pltpu.VMEM((1, CELLS), F32),
            pltpu.VMEM((2, FACES), jnp.int32),
            pltpu.VMEM((4, CAP), jnp.int32),
            pltpu.VMEM((5, CELLS, 2 * CELLS), BF16),
            pltpu.VMEM((STEPS, 40, CAP), F32),
            pltpu.VMEM((STEPS, 40, CAP), F32),
            pltpu.VMEM((CELLS, 1536), BF16),
            pltpu.VMEM((CELLS, 2048), BF16),
            pltpu.VMEM((4, CELLS, 2 * CAP), BF16),
            pltpu.VMEM((5, 8, FACES), F32),
            pltpu.VMEM((5, 8, FACES), F32),
            pltpu.VMEM((8, FACES), F32),
            pltpu.VMEM((2, 8, FACES), F32),
            pltpu.VMEM((4, 48, CAP), F32),
            pltpu.VMEM((4, 48, CAP), F32),
            pltpu.VMEM((2 * STEPS, 4, 40, CAP), F32),
            pltpu.VMEM((STEPS, 2, 40, CAP), F32),
            pltpu.VMEM((members, 8, CAP), F32),
            pltpu.VMEM((STEPS, members, 1, CAP), F32),
            dma((10,)),
            dma((4,)),
            dma((4,)),
            dma((2 * STEPS, 4)),
            dma((2 * STEPS, 4)),
            dma((STEPS, 2)),
            dma((STEPS, 2)),
            dma((2,)),
            dma((2,)),
            dma((STEPS, 2)),
            dma((STEPS, 2)),
        ],
        compiler_params=pltpu.CompilerParams(
            collective_id=0, has_side_effects=True, vmem_limit_bytes=60 * 2**20
        ),
    )(
        halves(krylov).reshape(NVEC * 40, CAP),
        halves(limiter),
        halves(pseudo_diag),
        face_states,
        face_angle[None],
        face_area[None],
        slope_weight[None],
        span_coupling[None],
        face_cells,
        send_list,
    )
    vectors = jnp.swapaxes(vectors.reshape(STEPS, 5, 2, 4, CAP), 2, 3)
    return vectors.reshape(STEPS, 5, 4, CELLS), hess


def solution(mesh):
    ns, nd = mesh.shape["span"], mesh.shape["dom"]
    ny = 4 if nd >= 16 else 2
    return jax.shard_map(
        functools.partial(on_device, (ns, ny, nd // ny)),
        mesh=mesh,
        in_specs=(
            P(None, None, "span", "dom"),
            P(None, "span", "dom"),
            P("span", "dom"),
            P(None, None, "span", "dom"),
            P("dom"),
            P("dom"),
            P("dom"),
            P("dom"),
            P(None, "dom"),
            P(None, "dom"),
            P(None, "dom"),
        ),
        out_specs=(P(None, None, "span", "dom"), P()),
        check_vma=False,
    )
```

```python
import functools

import jax
import jax.numpy as jnp
from jax import lax
from jax.experimental import pallas as pl
from jax.experimental.pallas import tpu as pltpu
from jax.sharding import PartitionSpec as P

MESH = pl.DeviceIdType.MESH
OFFSETS = (-2, -1, 1, 2)
NEAR = (1, 2, 0, 3)
EPSILON = 1e-06
F32 = jnp.float32
BF16 = jnp.bfloat16
STEPS = 3
NVEC = 20
CELLS = 256
FACES = 512
CAP = 128


def dot_nn(a, b):
    return lax.dot_general(a, b, (((1,), (0,)), ((), ())), preferred_element_type=F32)


def dot_nt(a, b):
    return lax.dot_general(a, b, (((1,), (1,)), ((), ())), preferred_element_type=F32)


def iota(shape, dim):
    return lax.broadcasted_iota(jnp.int32, shape, dim)


def top_rows(shape):
    return (iota(shape, 0) & 4) == 0


def flip(x):
    return pltpu.roll(x, 4, 0)


def split2(x):
    hi = x.astype(BF16).astype(F32)
    return jnp.concatenate([hi, x - hi], axis=0)


def split3(x):
    hi = x.astype(BF16).astype(F32)
    rest = x - hi
    mid = rest.astype(BF16).astype(F32)
    return jnp.concatenate([hi, mid, rest - mid], axis=0)


def operand(fields):
    both = split2(jnp.concatenate(fields, axis=0))
    top = top_rows(both.shape)
    return jnp.concatenate([jnp.where(top, both, 0.0), jnp.where(top, 0.0, both)], axis=1).astype(BF16)


def joined(y):
    half = y.shape[0] // 2
    return y[:half] + y[half:]


def packed_cells(y):
    out = []
    for v in range(5):
        low, high = y[8 * v : 8 * v + 8, :CAP], y[8 * v : 8 * v + 8, CAP:]
        top = top_rows(low.shape)
        out.append(jnp.where(top, low, high) + flip(jnp.where(top, high, low)))
    return out


def one_hot(size, row):
    return (iota((size, row.shape[1]), 0) == row).astype(F32)


def kernel(
    grid,
    count,
    k_any,
    lim_any,
    pd_any,
    fs_any,
    angle_any,
    area_any,
    weight_any,
    coupling_any,
    cells_any,
    sl_any,
    nv_ref,
    hess_ref,
    kv,
    limv,
    pdv,
    fsv,
    anglev,
    areav,
    weightv,
    couplingv,
    cellsv,
    slv,
    m_slope,
    sv,
    rv,
    w_own,
    w_sc,
    w_nb,
    cf_int,
    cf_gf,
    pl_int,
    pl_gf,
    msg_out,
    msg_in,
    nbuf,
    sbuf,
    gbuf,
    abuf,
    load_sem,
    msg_send,
    msg_recv,
    nb_send,
    nb_recv,
    sp_send,
    sp_recv,
    g_send,
    g_recv,
    a_send,
    a_recv,
    meet_y,
    meet_z,
):
    ns, ny, nz = grid
    nd = ny * nz
    s = lax.axis_index("span")
    d = lax.axis_index("dom")
    y, z = d // nz, lax.rem(d, nz)

    def dom_at(offset):
        return lax.rem(d + (offset + nd), nd)

    def span_at(offset):
        return lax.rem(s + (offset + ns), ns)

    xs = ns // 2
    x, core = s // 2, lax.rem(s, 2)
    places = (s * ny + y, z)
    sizes = (ns * ny, nz)
    starts = (0, ns * ny)

    def others(stage):
        if stage:
            hops = sorted(range(1, nz), key=lambda k: -min(k, nz - k))
            return [(s, y * nz + lax.rem(z + k, nz)) for k in hops]
        hops = [(i, c, k) for i in range(xs) for c in range(2) for k in range(ny)]
        hops = sorted(hops, key=lambda h: -(min(h[0], xs - h[0]) + min(h[2], ny - h[2])))
        return [
            (lax.rem(x + i, xs) * 2 + lax.rem(core + c, 2), lax.rem(y + k, ny) * nz + z)
            for i, c, k in hops
            if (i, c, k) != (0, 0, 0)
        ]

    barrier = pltpu.get_barrier_semaphore()
    near_z = [(s, y * nz + lax.rem(z + k, nz)) for k in (nz - 2, nz - 1, 1, 2)]
    near_y = [(s, lax.rem(y + k, ny) * nz + z) for k in range(1, ny)]
    partners = [(s, dom_at(o)) for o in OFFSETS] + near_z + near_y
    partners += [(lax.rem(s + k, ns), d) for k in range(1, ns)]
    for device in partners:
        pl.semaphore_signal(barrier, inc=1, device_id=device, device_id_type=MESH)

    def greet(semaphore, devices):
        for device in devices:
            pl.semaphore_signal(semaphore, inc=1, device_id=device, device_id_type=MESH)

    pairs = (
        (fs_any, fsv),
        (angle_any, anglev),
        (area_any, areav),
        (weight_any, weightv),
        (cells_any, cellsv),
        (sl_any, slv),
        (k_any, kv),
        (coupling_any, couplingv),
        (lim_any, limv),
        (pd_any, pdv),
    )
    loads = [pltpu.make_async_copy(src, dst, load_sem.at[i]) for i, (src, dst) in enumerate(pairs)]
    for load in loads:
        load.start()

    exists = [(d + o >= 0) & (d + o < nd) for o in OFFSETS]
    for j in range(4):

        @pl.when(jnp.logical_not(exists[j]))
        def _():
            msg_in[j] = jnp.zeros((48, CAP), F32)
            for number in range(2 * STEPS):
                nbuf[number, j] = jnp.zeros((40, CAP), F32)

    def when(condition, action):
        @pl.when(condition)
        def _():
            action()

    def send_field(src, number):
        copies = []
        for j in reversed(NEAR):
            copy = pltpu.make_async_remote_copy(
                src_ref=src,
                dst_ref=nbuf.at[number, 3 - j],
                send_sem=nb_send.at[number, j],
                recv_sem=nb_recv.at[number, 3 - j],
                device_id=(s, dom_at(OFFSETS[j])),
                device_id_type=MESH,
            )
            when(exists[j], copy.start)
            copies.append((j, copy))
        return dict(copies)

    def send_span(src, number):
        copies = []
        for side, offset in ((0, 1), (1, -1)):
            copy = pltpu.make_async_remote_copy(
                src_ref=src,
                dst_ref=sbuf.at[number, side],
                send_sem=sp_send.at[number, side],
                recv_sem=sp_recv.at[number, side],
                device_id=(span_at(offset), d),
                device_id_type=MESH,
            )
            copy.start()
            copies.append(copy)
        return copies

    unsent = []

    def sum_start(buf, send, recv, stage, value):
        place = buf.at[starts[stage] + places[stage]]
        buf[pl.ds(starts[stage] + places[stage], 1)] = value[None]
        for device in others(stage):
            pltpu.make_async_remote_copy(
                src_ref=place,
                dst_ref=place,
                send_sem=send.at[stage],
                recv_sem=recv.at[stage],
                device_id=device,
                device_id_type=MESH,
            ).start()
        span = buf.at[pl.ds(starts[stage], sizes[stage] - 1)]
        unsent.append(pltpu.make_async_copy(span, span, send.at[stage]).wait)

    def sum_finish(buf, recv, stage):
        n = sizes[stage]
        span = buf.at[pl.ds(starts[stage], n - 1)]
        pltpu.make_async_copy(span, span, recv.at[stage]).wait()
        terms = [buf[starts[stage] + k] for k in range(n)]
        while len(terms) > 1:
            terms = [sum(terms[i + 1 : i + 2], terms[i]) for i in range(0, len(terms), 2)]
        return terms[0]

    for load in loads[:5]:
        load.wait()
    angle, area, weight = anglev[...], areav[...], weightv[...]
    owner, other = cellsv[0:1, :], cellsv[1:2, :]
    nx, ny_ = jnp.cos(angle), jnp.sin(angle)
    state = [jnp.concatenate([fsv[0, v], fsv[1, v]], axis=0) for v in range(5)]
    inv = 1.0 / state[0]
    u1, u2, u3 = state[1] * inv, state[2] * inv, state[3] * inv
    pressure = 0.4 * (state[4] - 0.5 * (state[1] * u1 + state[2] * u2 + state[3] * u3))
    enthalpy = (state[4] + pressure) * inv
    speed = jnp.abs(u1 * nx + u2 * ny_) + jnp.sqrt(1.4 * pressure * inv)
    lam = jnp.maximum(speed, flip(speed))
    lam = jnp.where(top_rows(lam.shape), lam, -lam)
    half_area = 0.5 * area
    coefs = [u1, u2, u3, enthalpy, lam]
    for i, c in enumerate(coefs):
        cf_int[i] = c
    inside = (other < CELLS).astype(F32)
    pl_int[0:1, :] = nx
    pl_int[1:2, :] = ny_
    pl_int[2:3, :] = half_area * inside
    pl_int[3:4, :] = weight * inside
    pl_int[4:8, :] = jnp.zeros((4, FACES), F32)

    loads[5].wait()
    plane_rows = jnp.concatenate(
        [nx, ny_, half_area, weight, owner.astype(F32), jnp.zeros((3, FACES), F32)], axis=0
    )
    gathered = split3(jnp.concatenate([*coefs, plane_rows], axis=0)).astype(BF16)
    for j in range(4):
        slots = (iota((CAP, FACES), 0) + (CELLS + j * CAP) == other).astype(F32).astype(BF16)
        part = dot_nt(gathered, slots)
        part = part[0:48] + part[48:96] + part[96:144]
        msg_out[j, 0:45, :] = part[0:45]
        msg_out[j, 45:46, :] = slv[3 - j : 4 - j, :].astype(F32)
        msg_out[j, 46:48, :] = jnp.zeros((2, CAP), F32)

    pl.semaphore_wait(barrier, len(partners))

    first = send_field(k_any.at[pl.ds(40 * NVEC - 40, 40)], 0)
    messages = {}
    for j in reversed(NEAR):
        copy = pltpu.make_async_remote_copy(
            src_ref=msg_out.at[j],
            dst_ref=msg_in.at[j],
            send_sem=msg_send.at[j],
            recv_sem=msg_recv.at[j],
            device_id=(s, dom_at(OFFSETS[3 - j])),
            device_id_type=MESH,
        )
        when(exists[3 - j], copy.start)
        messages[j] = copy
    first_span = send_span(k_any.at[pl.ds(40 * NVEC - 40, 40)], 0)
    circle = near_y + [near_z[0], near_z[3]]
    greet(meet_y, circle)

    loads[6].wait()
    total = jnp.zeros((72, 72), F32)
    for pair in range(20):
        rows = jnp.concatenate(
            [kv[pl.ds(2 * pair + i, NVEC, stride=40), :] for i in range(2)], axis=1
        )
        rows = jnp.concatenate([rows, jnp.zeros((4, 2 * CAP), F32)], axis=0)
        rows = split3(rows).astype(BF16)
        total = total + dot_nt(rows, rows)
    rows = total[0:24] + total[24:48] + total[48:72]
    gram = rows[:, 0:24] + rows[:, 24:48] + rows[:, 48:72]
    gram = jnp.concatenate([gram, jnp.zeros((24, CAP - 24), F32)], axis=1)
    gram = gram[0:8] + pltpu.roll(gram[8:16], 32, 1) + pltpu.roll(gram[16:24], 64, 1)

    hot_a, hot_b = one_hot(CELLS, owner), one_hot(CELLS, other)
    w_own[:, 0:512] = (hot_a - hot_b).astype(BF16)
    w_sc[:, 0:512] = hot_a.astype(BF16)
    w_sc[:, 512:1024] = hot_b.astype(BF16)
    for j in range(4):
        at = 512 + j * CAP
        hot = one_hot(CELLS, msg_out[j, 44:45, :].astype(jnp.int32)).astype(BF16)
        w_own[:, at : at + CAP] = hot
        w_sc[:, at + 512 : at + 512 + CAP] = hot
        hot = one_hot(CELLS, slv[j : j + 1, :])
        w_own[:, at + 512 : at + 512 + CAP] = (-hot).astype(BF16)
        w_sc[:, at + 1024 : at + 1024 + CAP] = hot.astype(BF16)

    def near(own):
        return joined(dot_nn(operand(own), w_own[...]))

    first_near = near([kv[40 * NVEC - 40 :, :]])

    pl.semaphore_wait(meet_y, len(circle))
    far_z = [(s, y * nz + lax.rem(z + k, nz)) for k in (4, nz - 4)] if nz > 8 else []
    greet(meet_z, far_z)
    sum_start(gbuf, g_send, g_recv, 0, gram)

    for j in NEAR:
        when(exists[j], messages[j].wait_recv)
        at = j * CAP
        for i in range(5):
            mine, theirs = msg_out[j, 8 * i : 8 * i + 8, :], msg_in[j, 8 * i : 8 * i + 8, :]
            cf_gf[i, :, at : at + CAP] = jnp.where(top_rows(mine.shape), mine, theirs)
        for side, msg in ((0, msg_out), (1, msg_in)):
            pl_gf[side, :, at : at + CAP] = msg[j, 40:48, :]
        w_nb[j, :, 0:CAP] = (-one_hot(CELLS, msg_in[j, 45:46, :].astype(jnp.int32))).astype(BF16)
        w_nb[j, :, CAP:] = one_hot(CELLS, msg_in[j, 44:45, :].astype(jnp.int32)).astype(BF16)

    def jumps(near, number, copies):
        ghost = [None] * 4
        foreign = [None] * 4
        for j in NEAR:
            when(exists[j], copies[3 - j].wait_recv)
            part = joined(dot_nn(operand([nbuf[number, j]]), w_nb[j]))
            ghost[3 - j] = part[:, :CAP]
            foreign[j] = part[:, CAP:]
        return (
            near[:, 0:512],
            near[:, 512:1024] + jnp.concatenate(ghost, axis=1),
            near[:, 1024:1536] + jnp.concatenate(foreign, axis=1),
        )

    def transposed(e, cf, nx, ny, half_area):
        e = [half_area * x for x in e]
        u1, u2, u3, enthalpy, lam = (cf[i] for i in range(5))
        vn = u1 * nx + u2 * ny
        phi = 0.2 * (u1 * u1 + u2 * u2 + u3 * u3)
        cp = e[1] * nx + e[2] * ny + e[4] * vn
        ch = e[0] + e[1] * u1 + e[2] * u2 + e[3] * u3 + e[4] * enthalpy
        diag = vn + lam
        cp4 = 0.4 * cp
        return [
            e[0] * diag + cp * phi - ch * vn,
            e[1] * diag - u1 * cp4 + ch * nx,
            e[2] * diag - u2 * cp4 + ch * ny,
            e[3] * diag - u3 * cp4,
            e[4] * diag + cp4,
        ]

    def state_part(near, number, copies):
        e_int, e_gh, e_for = jumps(near, number, copies)
        jump_int, jump_gf = [], []
        for v in range(5):
            x = e_int[8 * v : 8 * v + 8]
            jump_int.append(x + flip(x))
            g, f = e_gh[8 * v : 8 * v + 8], e_for[8 * v : 8 * v + 8]
            top = top_rows(g.shape)
            jump_gf.append(jnp.where(top, g, f) + flip(jnp.where(top, f, g)))
        g_int = transposed(jump_int, cf_int, pl_int[0:1, :], pl_int[1:2, :], pl_int[2:3, :])
        top = top_rows((8, FACES))
        rows = [jnp.where(top, pl_gf[0, i : i + 1, :], pl_gf[1, i : i + 1, :]) for i in range(3)]
        g_gf = transposed(jump_gf, cf_gf, *rows)
        parts = []
        for g in (jnp.concatenate(g_int, axis=0), jnp.concatenate(g_gf, axis=0)):
            top = top_rows(g.shape)
            parts += [jnp.where(top, g, 0.0), jnp.where(top, 0.0, g)]
        lhs = split2(jnp.concatenate(parts, axis=1)).astype(BF16)
        return packed_cells(joined(dot_nt(lhs, w_sc[...])))

    def slope_matrices():
        def store(index, faces, weights, cells):
            hi = weights.astype(BF16)
            lo = (weights - hi.astype(F32)).astype(BF16)
            matrix = dot_nt(faces * hi, cells) + dot_nt(faces * lo, cells)
            hi = matrix.astype(BF16)
            m_slope[index, :, 0:CELLS] = hi
            m_slope[index, :, CELLS:] = (matrix - hi.astype(F32)).astype(BF16)

        for j in range(4):
            g, f = (3 - j) * CAP, j * CAP
            weights = jnp.concatenate([pl_gf[0, 3:4, g : g + CAP], pl_gf[1, 3:4, f : f + CAP]], axis=1)
            cells = jnp.concatenate(
                [w_own[:, 512 + g : 512 + g + CAP], w_own[:, 1024 + f : 1024 + f + CAP]], axis=1
            )
            store(j, w_nb[j], weights, cells)
        weights = jnp.concatenate([pl_int[3:4, :], pl_gf[0, 3:4, :], pl_gf[1, 3:4, :]], axis=1)
        store(4, w_own[...], weights, w_own[...])

    def slope_near(own):
        return dot_nn(operand(own), m_slope[4])

    def slope_part(total, number, copies):
        for j in NEAR:
            when(exists[j], copies[3 - j].wait_recv)
            total = total + dot_nn(operand([nbuf[number, j]]), m_slope[j])
        total = joined(total)
        return packed_cells(total[:, :CELLS] + total[:, CELLS:])

    row = iota((8, CAP), 0)
    layer = row & 3
    loads[7].wait()
    coupling = jnp.where(row < 4, couplingv[:, 0:CAP], couplingv[:, CAP:])
    eye = iota((24, CAP), 0) == iota((24, CAP), 1)
    row24 = iota((24, CAP), 0)

    def row_of(column):
        return jnp.sum(jnp.where(eye, column, 0.0), axis=0, keepdims=True)

    def local_sums(terms):
        rows = []
        for i in range(24):
            if i in terms:
                rows.append(jnp.sum(terms[i], axis=0, keepdims=True))
            else:
                rows.append(jnp.zeros((1, CAP), F32))
        return row_of(jnp.sum(jnp.concatenate(rows, axis=0), axis=1, keepdims=True))

    def product(a, b):
        out = a[0] * b[0]
        for v in range(1, 5):
            out = out + a[v] * b[v]
        return out

    def basis(i):
        return [kv[40 * i + 8 * v : 40 * i + 8 * v + 8, :] for v in range(5)]

    q = basis(NVEC - 1)
    copies, span_copies = first, first_span
    inverse = None
    done = []
    rr = None
    hess = []
    norms = []
    for m in range(STEPS):
        state_terms = state_part(near(q) if m else first_near, 2 * m, copies)
        if m == 0:
            loads[8].wait()
            loads[9].wait()
        slope_field = [limv[v] * state_terms[v] for v in range(5)]
        sv[m] = jnp.concatenate(slope_field, axis=0)
        slope_copies = send_field(sv.at[m], 2 * m + 1)
        if m == 0:
            slope_matrices()
            gram = sum_finish(gbuf, g_recv, 0)
            if far_z:
                pl.semaphore_wait(meet_z, len(far_z))
            sum_start(gbuf, g_send, g_recv, 1, gram)
        slope_own = slope_near(slope_field)
        for copy in span_copies:
            copy.wait_recv()
        local = []
        for v in range(5):
            above = jnp.where(layer == 0, pltpu.roll(sbuf[m, 0, 8 * v : 8 * v + 8, :], 5, 0), pltpu.roll(q[v], 1, 0))
            below = jnp.where(layer == 3, pltpu.roll(sbuf[m, 1, 8 * v : 8 * v + 8, :], 3, 0), pltpu.roll(q[v], 7, 0))
            local.append(
                pdv[...] * q[v] + coupling * (2.0 * q[v] - above - below) + state_terms[v]
            )
        slope_terms = slope_part(slope_own, 2 * m + 1, slope_copies)
        w = [local[v] - slope_terms[v] for v in range(5)]

        terms = {i: product(basis(i), w) for i in range(NVEC)}
        for i, vector in enumerate(done):
            terms[NVEC + i] = product(vector, w)
        if m:
            terms[NVEC + m - 1] = product(q, w)
            terms[22] = rr
        if m == STEPS - 1:
            terms[23] = product(w, w)
        value = local_sums(terms)
        sum_start(abuf.at[m], a_send.at[m], a_recv.at[m], 0, value)
        value = sum_finish(abuf.at[m], a_recv.at[m], 0)
        sum_start(abuf.at[m], a_send.at[m], a_recv.at[m], 1, value)
        if m == 0:
            gram = sum_finish(gbuf, g_recv, 1) / count
            wide = jnp.concatenate(
                [gram, pltpu.roll(gram, CAP - 32, 1), pltpu.roll(gram, CAP - 64, 1)], axis=0
            )
            lane = iota((24, CAP), 1)
            kept = (lane < NVEC) & (row24 < NVEC)
            diagonal = (row24 == lane) & (row24 >= NVEC)
            gram_mean = jnp.where(kept, wide, 0.0)
            work = gram_mean + jnp.where(diagonal | (lane == row24 + 32), 1.0, 0.0)
            for k in range(NVEC):
                column = jnp.sum(jnp.where(lane == k, work, 0.0), axis=1, keepdims=True)
                pivot = work[k : k + 1, :]
                scale = 1.0 / column[k : k + 1, :]
                work = work - (column - jnp.where(row24[:, 0:1] == k, 1.0, 0.0)) * (pivot * scale)
            inverse = pltpu.roll(work, CAP - 32, 1)
        value = sum_finish(abuf.at[m], a_recv.at[m], 1)
        value = value / count
        solved = jnp.sum(inverse * value, axis=1, keepdims=True)
        if m:
            norms.append(solved[22:23, :])
            ww = solved[23:24, :]
            beta = jnp.sqrt(norms[-1] + EPSILON)
            scale = 1.0 / beta
            last = [x * scale for x in q]
            nv_ref[m - 1] = jnp.concatenate(last, axis=0)
            done.append(last)
            hess[-1] = jnp.where(iota((1, CAP), 1) == 22, beta, hess[-1])
            w = [x * scale for x in w]
            solved = solved * scale
            solved = jnp.where(row24[:, 0:1] == NVEC + m - 1, solved * scale, solved)
            if m == 1:
                across = solved[20:21, :]
        hess.append(jnp.where(iota((1, CAP), 1) < NVEC + m, row_of(solved), 0.0))
        wide = jnp.broadcast_to(solved, (24, CAP))
        r = w
        for i in range(NVEC + m):
            c = wide[i : i + 1, :]
            vector = basis(i) if i < NVEC else done[i - NVEC]
            r = [r[v] - c * vector[v] for v in range(5)]
        rv[m] = jnp.concatenate(r, axis=0)
        unsent += [functools.partial(when, exists[j], c.wait_send) for j, c in slope_copies.items()]
        if m + 1 < STEPS:
            copies = send_field(rv.at[m], 2 * m + 2)
            span_copies = send_span(rv.at[m], m + 1)
            unsent += [functools.partial(when, exists[j], c.wait_send) for j, c in copies.items()]
            unsent += [c.wait_send for c in span_copies]
            rr = product(r, r)
        q = r

    n0, n1 = (n / (n + EPSILON) for n in norms)
    cross = across * (1.0 - n0) / jnp.sqrt(norms[1] + EPSILON)
    lane = iota((24, CAP), 1)
    whole = gram_mean + jnp.where((row24 == 20) & (lane == 20), n0, 0.0)
    whole = whole + jnp.where((row24 == 21) & (lane == 21), n1, 0.0)
    whole = whole + jnp.where((row24 + lane == 41) & (row24 >= 20) & (lane >= 20), cross, 0.0)
    c_row = row_of(jnp.where(row24[:, 0:1] < 22, solved, 0.0))
    p_row = value * scale
    p_row = jnp.where(iota((1, CAP), 1) == 21, p_row * scale, p_row)
    inner = jnp.sum(whole * c_row - jnp.where(eye, 2.0 * p_row, 0.0), axis=1, keepdims=True)
    inner = jnp.where(row24[:, 0:1] < 22, inner * solved, 0.0)
    rr = ww * scale * scale + jnp.sum(inner, axis=0, keepdims=True)
    beta = jnp.sqrt(jnp.maximum(rr, 0.0) + EPSILON)
    scale = 1.0 / beta
    nv_ref[STEPS - 1] = jnp.concatenate([x * scale for x in q], axis=0)
    hess[-1] = jnp.where(iota((1, CAP), 1) == 22, beta, hess[-1])
    hess_ref[...] = jnp.concatenate(hess, axis=0)[:, 0:23]

    for j in range(4):
        when(exists[j], first[j].wait_send)
        when(exists[3 - j], messages[j].wait_send)
    for c in first_span:
        c.wait_send()
    for wait in unsent:
        wait()


def on_device(grid, krylov, limiter, pseudo_diag, face_states, face_angle, face_area, slope_weight,
              span_coupling, face_cells, send_list, send_count):
    ns, ny, nz = grid
    count = float(5 * 4 * CELLS * ns * ny * nz)

    def halves(x):
        lead = x.shape[:-2]
        x = x.reshape(*lead, 4, 2, CAP)
        return jnp.swapaxes(x, -3, -2).reshape(*lead, 8, CAP)

    anywhere = pl.BlockSpec(memory_space=pl.ANY)
    members = ns * ny + nz
    dma = pltpu.SemaphoreType.DMA
    vectors, hess = pl.pallas_call(
        functools.partial(kernel, grid, count),
        out_shape=(
            pltpu.VMEM((STEPS, 40, CAP), F32),
            pltpu.VMEM((STEPS, 23), F32),
        ),
        in_specs=[anywhere] * 10,
        out_specs=(pl.BlockSpec(memory_space=pltpu.VMEM),) * 2,
        scratch_shapes=[
            pltpu.VMEM((NVEC * 40, CAP), F32),
            pltpu.VMEM((5, 8, CAP), F32),
            pltpu.VMEM((8, CAP), F32),
            pltpu.VMEM((2, 5, 4, FACES), F32),
            pltpu.VMEM((1, FACES), F32),
            pltpu.VMEM((1, FACES), F32),
            pltpu.VMEM((1, FACES), F32),
            pltpu.VMEM((1, CELLS), F32),
            pltpu.VMEM((2, FACES), jnp.int32),
            pltpu.VMEM((4, CAP), jnp.int32),
            pltpu.VMEM((5, CELLS, 2 * CELLS), BF16),
            pltpu.VMEM((STEPS, 40, CAP), F32),
            pltpu.VMEM((STEPS, 40, CAP), F32),
            pltpu.VMEM((CELLS, 1536), BF16),
            pltpu.VMEM((CELLS, 2048), BF16),
            pltpu.VMEM((4, CELLS, 2 * CAP), BF16),
            pltpu.VMEM((5, 8, FACES), F32),
            pltpu.VMEM((5, 8, FACES), F32),
            pltpu.VMEM((8, FACES), F32),
            pltpu.VMEM((2, 8, FACES), F32),
            pltpu.VMEM((4, 48, CAP), F32),
            pltpu.VMEM((4, 48, CAP), F32),
            pltpu.VMEM((2 * STEPS, 4, 40, CAP), F32),
            pltpu.VMEM((STEPS, 2, 40, CAP), F32),
            pltpu.VMEM((members, 8, CAP), F32),
            pltpu.VMEM((STEPS, members, 1, CAP), F32),
            dma((10,)),
            dma((4,)),
            dma((4,)),
            dma((2 * STEPS, 4)),
            dma((2 * STEPS, 4)),
            dma((STEPS, 2)),
            dma((STEPS, 2)),
            dma((2,)),
            dma((2,)),
            dma((STEPS, 2)),
            dma((STEPS, 2)),
            pltpu.SemaphoreType.REGULAR,
            pltpu.SemaphoreType.REGULAR,
        ],
        compiler_params=pltpu.CompilerParams(
            collective_id=0, has_side_effects=True, vmem_limit_bytes=60 * 2**20
        ),
    )(
        halves(krylov).reshape(NVEC * 40, CAP),
        halves(limiter),
        halves(pseudo_diag),
        face_states,
        face_angle[None],
        face_area[None],
        slope_weight[None],
        span_coupling[None],
        face_cells,
        send_list,
    )
    vectors = jnp.swapaxes(vectors.reshape(STEPS, 5, 2, 4, CAP), 2, 3)
    return vectors.reshape(STEPS, 5, 4, CELLS), hess


def solution(mesh):
    ns, nd = mesh.shape["span"], mesh.shape["dom"]
    ny = 4 if nd >= 16 else 2
    return jax.shard_map(
        functools.partial(on_device, (ns, ny, nd // ny)),
        mesh=mesh,
        in_specs=(
            P(None, None, "span", "dom"),
            P(None, "span", "dom"),
            P("span", "dom"),
            P(None, None, "span", "dom"),
            P("dom"),
            P("dom"),
            P("dom"),
            P("dom"),
            P(None, "dom"),
            P(None, "dom"),
            P(None, "dom"),
        ),
        out_specs=(P(None, None, "span", "dom"), P()),
        check_vma=False,
    )
```

```python
import functools

import jax
import jax.numpy as jnp
from jax import lax
from jax.experimental import pallas as pl
from jax.experimental.pallas import tpu as pltpu
from jax.sharding import PartitionSpec as P

MESH = pl.DeviceIdType.MESH
OFFSETS = (-2, -1, 1, 2)
NEAR = (1, 2, 0, 3)
PACE = (0, 2, 5, 7, 10, 13, 16, 19, 20)
EPSILON = 1e-06
F32 = jnp.float32
BF16 = jnp.bfloat16
STEPS = 3
NVEC = 20
CELLS = 256
FACES = 512
CAP = 128


def dot_nn(a, b):
    return lax.dot_general(a, b, (((1,), (0,)), ((), ())), preferred_element_type=F32)


def dot_nt(a, b):
    return lax.dot_general(a, b, (((1,), (1,)), ((), ())), preferred_element_type=F32)


def iota(shape, dim):
    return lax.broadcasted_iota(jnp.int32, shape, dim)


def top_rows(shape):
    return (iota(shape, 0) & 4) == 0


def flip(x):
    return pltpu.roll(x, 4, 0)


def split2(x):
    hi = x.astype(BF16).astype(F32)
    return jnp.concatenate([hi, x - hi], axis=0)


def split3(x):
    hi = x.astype(BF16).astype(F32)
    rest = x - hi
    mid = rest.astype(BF16).astype(F32)
    return jnp.concatenate([hi, mid, rest - mid], axis=0)


def operand(fields):
    both = split2(jnp.concatenate(fields, axis=0))
    top = top_rows(both.shape)
    return jnp.concatenate([jnp.where(top, both, 0.0), jnp.where(top, 0.0, both)], axis=1).astype(BF16)


def joined(y):
    half = y.shape[0] // 2
    return y[:half] + y[half:]


def packed_cells(y):
    out = []
    for v in range(5):
        low, high = y[8 * v : 8 * v + 8, :CAP], y[8 * v : 8 * v + 8, CAP:]
        top = top_rows(low.shape)
        out.append(jnp.where(top, low, high) + flip(jnp.where(top, high, low)))
    return out


def one_hot(size, row):
    return (iota((size, row.shape[1]), 0) == row).astype(F32)


def kernel(
    grid,
    count,
    k_any,
    lim_any,
    pd_any,
    fs_any,
    angle_any,
    area_any,
    weight_any,
    coupling_any,
    cells_any,
    sl_any,
    nv_ref,
    hess_ref,
    kv,
    limv,
    pdv,
    fsv,
    anglev,
    areav,
    weightv,
    couplingv,
    cellsv,
    slv,
    m_slope,
    sv,
    rv,
    w_own,
    w_sc,
    w_nb,
    cf_int,
    cf_gf,
    pl_int,
    pl_gf,
    msg_out,
    msg_in,
    nbuf,
    sbuf,
    gbuf,
    abuf,
    load_sem,
    msg_send,
    msg_recv,
    nb_send,
    nb_recv,
    sp_send,
    sp_recv,
    g_send,
    g_recv,
    a_send,
    a_recv,
    meet_y,
    meet_z,
    far_kv,
    wv,
    far_w,
    far_r,
    kv_send,
    kv_recv,
    w_send,
    w_recv,
):
    ns, ny, nz = grid
    nd = ny * nz
    s = lax.axis_index("span")
    d = lax.axis_index("dom")
    y, z = d // nz, lax.rem(d, nz)

    def dom_at(offset):
        return lax.rem(d + (offset + nd), nd)

    def span_at(offset):
        return lax.rem(s + (offset + ns), ns)

    xs = ns // 2
    x, core = s // 2, lax.rem(s, 2)
    places = (s * ny + y, z)
    sizes = (ns * ny, nz)
    starts = (0, ns * ny)

    def others(stage):
        if stage:
            hops = sorted(range(1, nz), key=lambda k: -min(k, nz - k))
            return [(s, y * nz + lax.rem(z + k, nz)) for k in hops]
        hops = [(i, c, k) for i in range(xs) for c in range(2) for k in range(ny)]
        hops = sorted(hops, key=lambda h: -(min(h[0], xs - h[0]) + min(h[2], ny - h[2])))
        return [
            (lax.rem(x + i, xs) * 2 + lax.rem(core + c, 2), lax.rem(y + k, ny) * nz + z)
            for i, c, k in hops
            if (i, c, k) != (0, 0, 0)
        ]

    barrier = pltpu.get_barrier_semaphore()
    near_z = [(s, y * nz + lax.rem(z + k, nz)) for k in (nz - 2, nz - 1, 1, 2)]
    near_y = [(s, lax.rem(y + k, ny) * nz + z) for k in range(1, ny)]
    partners = [(s, dom_at(o)) for o in OFFSETS] + near_z + near_y
    partners += [(lax.rem(s + k, ns), d) for k in range(1, ns)]
    for device in partners:
        pl.semaphore_signal(barrier, inc=1, device_id=device, device_id_type=MESH)

    def greet(semaphore, devices):
        for device in devices:
            pl.semaphore_signal(semaphore, inc=1, device_id=device, device_id_type=MESH)

    pairs = (
        (fs_any, fsv),
        (angle_any, anglev),
        (area_any, areav),
        (weight_any, weightv),
        (cells_any, cellsv),
        (sl_any, slv),
        (k_any, kv),
        (coupling_any, couplingv),
        (lim_any, limv),
        (pd_any, pdv),
    )
    loads = [pltpu.make_async_copy(src, dst, load_sem.at[i]) for i, (src, dst) in enumerate(pairs)]
    for load in loads:
        load.start()

    exists = [(d + o >= 0) & (d + o < nd) for o in OFFSETS]
    for j in range(4):

        @pl.when(jnp.logical_not(exists[j]))
        def _():
            msg_in[j] = jnp.zeros((48, CAP), F32)
            for number in range(2 * STEPS):
                nbuf[number, j] = jnp.zeros((40, CAP), F32)
            far_kv[j] = jnp.zeros((NVEC * 40, CAP), F32)
            far_w[j] = jnp.zeros((40, CAP), F32)

    def when(condition, action):
        @pl.when(condition)
        def _():
            action()

    def send_field(src, number):
        copies = []
        for j in reversed(NEAR):
            copy = pltpu.make_async_remote_copy(
                src_ref=src,
                dst_ref=nbuf.at[number, 3 - j],
                send_sem=nb_send.at[number, j],
                recv_sem=nb_recv.at[number, 3 - j],
                device_id=(s, dom_at(OFFSETS[j])),
                device_id_type=MESH,
            )
            when(exists[j], copy.start)
            copies.append((j, copy))
        return dict(copies)

    def send_span(src, number):
        copies = []
        for side, offset in ((0, 1), (1, -1)):
            copy = pltpu.make_async_remote_copy(
                src_ref=src,
                dst_ref=sbuf.at[number, side],
                send_sem=sp_send.at[number, side],
                recv_sem=sp_recv.at[number, side],
                device_id=(span_at(offset), d),
                device_id_type=MESH,
            )
            copy.start()
            copies.append(copy)
        return copies

    unsent = []

    def send_basis(part):
        low, high = PACE[part], PACE[part + 1]
        rows = pl.ds(40 * low, 40 * (high - low))
        for j in reversed(NEAR):
            copy = pltpu.make_async_remote_copy(
                src_ref=kv.at[rows],
                dst_ref=far_kv.at[3 - j, rows],
                send_sem=kv_send.at[j],
                recv_sem=kv_recv.at[3 - j],
                device_id=(s, dom_at(OFFSETS[j])),
                device_id_type=MESH,
            )
            when(exists[j], copy.start)

    def send_product():
        copies = {}
        for j in reversed(NEAR):
            copies[j] = pltpu.make_async_remote_copy(
                src_ref=wv,
                dst_ref=far_w.at[3 - j],
                send_sem=w_send.at[j],
                recv_sem=w_recv.at[3 - j],
                device_id=(s, dom_at(OFFSETS[j])),
                device_id_type=MESH,
            )
            when(exists[j], copies[j].start)
        return copies


    def sum_start(buf, send, recv, stage, value):
        place = buf.at[starts[stage] + places[stage]]
        buf[pl.ds(starts[stage] + places[stage], 1)] = value[None]
        for device in others(stage):
            pltpu.make_async_remote_copy(
                src_ref=place,
                dst_ref=place,
                send_sem=send.at[stage],
                recv_sem=recv.at[stage],
                device_id=device,
                device_id_type=MESH,
            ).start()
        span = buf.at[pl.ds(starts[stage], sizes[stage] - 1)]
        unsent.append(pltpu.make_async_copy(span, span, send.at[stage]).wait)

    def sum_finish(buf, recv, stage):
        n = sizes[stage]
        span = buf.at[pl.ds(starts[stage], n - 1)]
        pltpu.make_async_copy(span, span, recv.at[stage]).wait()
        terms = [buf[starts[stage] + k] for k in range(n)]
        while len(terms) > 1:
            terms = [sum(terms[i + 1 : i + 2], terms[i]) for i in range(0, len(terms), 2)]
        return terms[0]

    for load in loads[:5]:
        load.wait()
    angle, area, weight = anglev[...], areav[...], weightv[...]
    owner, other = cellsv[0:1, :], cellsv[1:2, :]
    nx, ny_ = jnp.cos(angle), jnp.sin(angle)
    state = [jnp.concatenate([fsv[0, v], fsv[1, v]], axis=0) for v in range(5)]
    inv = 1.0 / state[0]
    u1, u2, u3 = state[1] * inv, state[2] * inv, state[3] * inv
    pressure = 0.4 * (state[4] - 0.5 * (state[1] * u1 + state[2] * u2 + state[3] * u3))
    enthalpy = (state[4] + pressure) * inv
    speed = jnp.abs(u1 * nx + u2 * ny_) + jnp.sqrt(1.4 * pressure * inv)
    lam = jnp.maximum(speed, flip(speed))
    lam = jnp.where(top_rows(lam.shape), lam, -lam)
    half_area = 0.5 * area
    coefs = [u1, u2, u3, enthalpy, lam]
    for i, c in enumerate(coefs):
        cf_int[i] = c
    inside = (other < CELLS).astype(F32)
    pl_int[0:1, :] = nx
    pl_int[1:2, :] = ny_
    pl_int[2:3, :] = half_area * inside
    pl_int[3:4, :] = weight * inside
    pl_int[4:8, :] = jnp.zeros((4, FACES), F32)

    loads[5].wait()
    plane_rows = jnp.concatenate(
        [nx, ny_, half_area, weight, owner.astype(F32), jnp.zeros((3, FACES), F32)], axis=0
    )
    gathered = split3(jnp.concatenate([*coefs, plane_rows], axis=0)).astype(BF16)
    for j in range(4):
        slots = (iota((CAP, FACES), 0) + (CELLS + j * CAP) == other).astype(F32).astype(BF16)
        part = dot_nt(gathered, slots)
        part = part[0:48] + part[48:96] + part[96:144]
        msg_out[j, 0:45, :] = part[0:45]
        msg_out[j, 45:46, :] = slv[3 - j : 4 - j, :].astype(F32)
        msg_out[j, 46:48, :] = jnp.zeros((2, CAP), F32)

    pl.semaphore_wait(barrier, len(partners))

    first = send_field(k_any.at[pl.ds(40 * NVEC - 40, 40)], 0)
    messages = {}
    for j in reversed(NEAR):
        copy = pltpu.make_async_remote_copy(
            src_ref=msg_out.at[j],
            dst_ref=msg_in.at[j],
            send_sem=msg_send.at[j],
            recv_sem=msg_recv.at[j],
            device_id=(s, dom_at(OFFSETS[3 - j])),
            device_id_type=MESH,
        )
        when(exists[3 - j], copy.start)
        messages[j] = copy
    first_span = send_span(k_any.at[pl.ds(40 * NVEC - 40, 40)], 0)
    circle = near_y + [near_z[0], near_z[3]]
    greet(meet_y, circle)

    loads[6].wait()
    send_basis(0)
    total = jnp.zeros((72, 72), F32)
    for pair in range(20):
        rows = jnp.concatenate(
            [kv[pl.ds(2 * pair + i, NVEC, stride=40), :] for i in range(2)], axis=1
        )
        rows = jnp.concatenate([rows, jnp.zeros((4, 2 * CAP), F32)], axis=0)
        rows = split3(rows).astype(BF16)
        total = total + dot_nt(rows, rows)
    rows = total[0:24] + total[24:48] + total[48:72]
    gram = rows[:, 0:24] + rows[:, 24:48] + rows[:, 48:72]
    gram = jnp.concatenate([gram, jnp.zeros((24, CAP - 24), F32)], axis=1)
    gram = gram[0:8] + pltpu.roll(gram[8:16], 32, 1) + pltpu.roll(gram[16:24], 64, 1)

    hot_a, hot_b = one_hot(CELLS, owner), one_hot(CELLS, other)
    w_own[:, 0:512] = (hot_a - hot_b).astype(BF16)
    w_sc[:, 0:512] = hot_a.astype(BF16)
    w_sc[:, 512:1024] = hot_b.astype(BF16)
    for j in range(4):
        at = 512 + j * CAP
        hot = one_hot(CELLS, msg_out[j, 44:45, :].astype(jnp.int32)).astype(BF16)
        w_own[:, at : at + CAP] = hot
        w_sc[:, at + 512 : at + 512 + CAP] = hot
        hot = one_hot(CELLS, slv[j : j + 1, :])
        w_own[:, at + 512 : at + 512 + CAP] = (-hot).astype(BF16)
        w_sc[:, at + 1024 : at + 1024 + CAP] = hot.astype(BF16)

    def near(own):
        return joined(dot_nn(operand(own), w_own[...]))

    first_near = near([kv[40 * NVEC - 40 :, :]])

    pl.semaphore_wait(meet_y, len(circle))
    far_z = [(s, y * nz + lax.rem(z + k, nz)) for k in (4, nz - 4)] if nz > 8 else []
    greet(meet_z, far_z)
    sum_start(gbuf, g_send, g_recv, 0, gram)

    for j in NEAR:
        when(exists[j], messages[j].wait_recv)
        at = j * CAP
        for i in range(5):
            mine, theirs = msg_out[j, 8 * i : 8 * i + 8, :], msg_in[j, 8 * i : 8 * i + 8, :]
            cf_gf[i, :, at : at + CAP] = jnp.where(top_rows(mine.shape), mine, theirs)
        for side, msg in ((0, msg_out), (1, msg_in)):
            pl_gf[side, :, at : at + CAP] = msg[j, 40:48, :]
        w_nb[j, :, 0:CAP] = (-one_hot(CELLS, msg_in[j, 45:46, :].astype(jnp.int32))).astype(BF16)
        w_nb[j, :, CAP:] = one_hot(CELLS, msg_in[j, 44:45, :].astype(jnp.int32)).astype(BF16)

    def jumps(near, number, copies):
        ghost = [None] * 4
        foreign = [None] * 4
        for j in NEAR:
            if copies is None:
                block = far_r[j]
            else:
                when(exists[j], copies[3 - j].wait_recv)
                block = nbuf[number, j]
            part = joined(dot_nn(operand([block]), w_nb[j]))
            ghost[3 - j] = part[:, :CAP]
            foreign[j] = part[:, CAP:]
        return (
            near[:, 0:512],
            near[:, 512:1024] + jnp.concatenate(ghost, axis=1),
            near[:, 1024:1536] + jnp.concatenate(foreign, axis=1),
        )

    def transposed(e, cf, nx, ny, half_area):
        e = [half_area * x for x in e]
        u1, u2, u3, enthalpy, lam = (cf[i] for i in range(5))
        vn = u1 * nx + u2 * ny
        phi = 0.2 * (u1 * u1 + u2 * u2 + u3 * u3)
        cp = e[1] * nx + e[2] * ny + e[4] * vn
        ch = e[0] + e[1] * u1 + e[2] * u2 + e[3] * u3 + e[4] * enthalpy
        diag = vn + lam
        cp4 = 0.4 * cp
        return [
            e[0] * diag + cp * phi - ch * vn,
            e[1] * diag - u1 * cp4 + ch * nx,
            e[2] * diag - u2 * cp4 + ch * ny,
            e[3] * diag - u3 * cp4,
            e[4] * diag + cp4,
        ]

    def state_part(near, number, copies):
        e_int, e_gh, e_for = jumps(near, number, copies)
        jump_int, jump_gf = [], []
        for v in range(5):
            x = e_int[8 * v : 8 * v + 8]
            jump_int.append(x + flip(x))
            g, f = e_gh[8 * v : 8 * v + 8], e_for[8 * v : 8 * v + 8]
            top = top_rows(g.shape)
            jump_gf.append(jnp.where(top, g, f) + flip(jnp.where(top, f, g)))
        g_int = transposed(jump_int, cf_int, pl_int[0:1, :], pl_int[1:2, :], pl_int[2:3, :])
        top = top_rows((8, FACES))
        rows = [jnp.where(top, pl_gf[0, i : i + 1, :], pl_gf[1, i : i + 1, :]) for i in range(3)]
        g_gf = transposed(jump_gf, cf_gf, *rows)
        parts = []
        for g in (jnp.concatenate(g_int, axis=0), jnp.concatenate(g_gf, axis=0)):
            top = top_rows(g.shape)
            parts += [jnp.where(top, g, 0.0), jnp.where(top, 0.0, g)]
        lhs = split2(jnp.concatenate(parts, axis=1)).astype(BF16)
        return packed_cells(joined(dot_nt(lhs, w_sc[...])))

    def slope_matrices():
        def store(index, faces, weights, cells):
            hi = weights.astype(BF16)
            lo = (weights - hi.astype(F32)).astype(BF16)
            matrix = dot_nt(faces * hi, cells) + dot_nt(faces * lo, cells)
            hi = matrix.astype(BF16)
            m_slope[index, :, 0:CELLS] = hi
            m_slope[index, :, CELLS:] = (matrix - hi.astype(F32)).astype(BF16)

        for j in range(4):
            g, f = (3 - j) * CAP, j * CAP
            weights = jnp.concatenate([pl_gf[0, 3:4, g : g + CAP], pl_gf[1, 3:4, f : f + CAP]], axis=1)
            cells = jnp.concatenate(
                [w_own[:, 512 + g : 512 + g + CAP], w_own[:, 1024 + f : 1024 + f + CAP]], axis=1
            )
            store(j, w_nb[j], weights, cells)
        weights = jnp.concatenate([pl_int[3:4, :], pl_gf[0, 3:4, :], pl_gf[1, 3:4, :]], axis=1)
        store(4, w_own[...], weights, w_own[...])

    def slope_near(own):
        return dot_nn(operand(own), m_slope[4])

    def slope_part(total, number, copies):
        for j in NEAR:
            when(exists[j], copies[3 - j].wait_recv)
            total = total + dot_nn(operand([nbuf[number, j]]), m_slope[j])
        total = joined(total)
        return packed_cells(total[:, :CELLS] + total[:, CELLS:])

    def far_residual(j, copies, scale, wide):
        when(exists[j], copies[3 - j].wait_recv)
        arrived = pltpu.make_async_copy(far_kv.at[j], far_kv.at[j], kv_recv.at[j])
        when(exists[j], arrived.wait)
        out = []
        for v in range(5):
            rows = slice(8 * v, 8 * v + 8)
            r = far_w[j, rows, :] * scale
            for i in range(NVEC):
                r = r - wide[i : i + 1, :] * far_kv[j, 40 * i + 8 * v : 40 * i + 8 * v + 8, :]
            out.append(r - wide[NVEC : NVEC + 1, :] * (nbuf[2, j, rows, :] * scale))
        return jnp.concatenate(out, axis=0)

    row = iota((8, CAP), 0)
    layer = row & 3
    loads[7].wait()
    coupling = jnp.where(row < 4, couplingv[:, 0:CAP], couplingv[:, CAP:])
    eye = iota((24, CAP), 0) == iota((24, CAP), 1)
    row24 = iota((24, CAP), 0)

    def row_of(column):
        return jnp.sum(jnp.where(eye, column, 0.0), axis=0, keepdims=True)

    def local_sums(terms):
        rows = []
        for i in range(24):
            if i in terms:
                rows.append(jnp.sum(terms[i], axis=0, keepdims=True))
            else:
                rows.append(jnp.zeros((1, CAP), F32))
        return row_of(jnp.sum(jnp.concatenate(rows, axis=0), axis=1, keepdims=True))

    def product(a, b):
        out = a[0] * b[0]
        for v in range(1, 5):
            out = out + a[v] * b[v]
        return out

    def basis(i):
        return [kv[40 * i + 8 * v : 40 * i + 8 * v + 8, :] for v in range(5)]

    q = basis(NVEC - 1)
    copies, span_copies = first, first_span
    inverse = None
    done = []
    rr = None
    hess = []
    norms = []
    for m in range(STEPS):
        state_terms = state_part(near(q) if m else first_near, 2 * m, copies)
        if m == 0:
            loads[8].wait()
            loads[9].wait()
        slope_field = [limv[v] * state_terms[v] for v in range(5)]
        sv[m] = jnp.concatenate(slope_field, axis=0)
        slope_copies = send_field(sv.at[m], 2 * m + 1)
        if m < 2:
            send_basis(4 * m + 1)
        if m == 0:
            slope_matrices()
            gram = sum_finish(gbuf, g_recv, 0)
            if far_z:
                pl.semaphore_wait(meet_z, len(far_z))
            sum_start(gbuf, g_send, g_recv, 1, gram)
        slope_own = slope_near(slope_field)
        for copy in span_copies:
            copy.wait_recv()
        local = []
        for v in range(5):
            above = jnp.where(layer == 0, pltpu.roll(sbuf[m, 0, 8 * v : 8 * v + 8, :], 5, 0), pltpu.roll(q[v], 1, 0))
            below = jnp.where(layer == 3, pltpu.roll(sbuf[m, 1, 8 * v : 8 * v + 8, :], 3, 0), pltpu.roll(q[v], 7, 0))
            local.append(
                pdv[...] * q[v] + coupling * (2.0 * q[v] - above - below) + state_terms[v]
            )
        slope_terms = slope_part(slope_own, 2 * m + 1, slope_copies)
        w = [local[v] - slope_terms[v] for v in range(5)]

        terms = {i: product(basis(i), w) for i in range(NVEC)}
        for i, vector in enumerate(done):
            terms[NVEC + i] = product(vector, w)
        if m:
            terms[NVEC + m - 1] = product(q, w)
            terms[22] = rr
        if m == STEPS - 1:
            terms[23] = product(w, w)
        value = local_sums(terms)
        sum_start(abuf.at[m], a_send.at[m], a_recv.at[m], 0, value)
        if m == 1:
            wv[...] = jnp.concatenate(w, axis=0)
            product_copies = send_product()
            unsent += [functools.partial(when, exists[j], c.wait_send) for j, c in product_copies.items()]
        if m < 2:
            send_basis(4 * m + 2)
        value = sum_finish(abuf.at[m], a_recv.at[m], 0)
        sum_start(abuf.at[m], a_send.at[m], a_recv.at[m], 1, value)
        if m < 2:
            send_basis(4 * m + 3)
        if m == 0:
            gram = sum_finish(gbuf, g_recv, 1) / count
            wide = jnp.concatenate(
                [gram, pltpu.roll(gram, CAP - 32, 1), pltpu.roll(gram, CAP - 64, 1)], axis=0
            )
            lane = iota((24, CAP), 1)
            kept = (lane < NVEC) & (row24 < NVEC)
            diagonal = (row24 == lane) & (row24 >= NVEC)
            gram_mean = jnp.where(kept, wide, 0.0)
            work = gram_mean + jnp.where(diagonal | (lane == row24 + 32), 1.0, 0.0)
            for k in range(NVEC):
                column = jnp.sum(jnp.where(lane == k, work, 0.0), axis=1, keepdims=True)
                pivot = work[k : k + 1, :]
                scale = 1.0 / column[k : k + 1, :]
                work = work - (column - jnp.where(row24[:, 0:1] == k, 1.0, 0.0)) * (pivot * scale)
            inverse = pltpu.roll(work, CAP - 32, 1)
        value = sum_finish(abuf.at[m], a_recv.at[m], 1)
        value = value / count
        solved = jnp.sum(inverse * value, axis=1, keepdims=True)
        if m:
            norms.append(solved[22:23, :])
            ww = solved[23:24, :]
            beta = jnp.sqrt(norms[-1] + EPSILON)
            scale = 1.0 / beta
            last = [x * scale for x in q]
            nv_ref[m - 1] = jnp.concatenate(last, axis=0)
            done.append(last)
            hess[-1] = jnp.where(iota((1, CAP), 1) == 22, beta, hess[-1])
            w = [x * scale for x in w]
            solved = solved * scale
            solved = jnp.where(row24[:, 0:1] == NVEC + m - 1, solved * scale, solved)
            if m == 1:
                across = solved[20:21, :]
        hess.append(jnp.where(iota((1, CAP), 1) < NVEC + m, row_of(solved), 0.0))
        wide = jnp.broadcast_to(solved, (24, CAP))
        r = w
        for i in range(NVEC + m):
            c = wide[i : i + 1, :]
            vector = basis(i) if i < NVEC else done[i - NVEC]
            r = [r[v] - c * vector[v] for v in range(5)]
        rv[m] = jnp.concatenate(r, axis=0)
        unsent += [functools.partial(when, exists[j], c.wait_send) for j, c in slope_copies.items()]
        if m + 1 < STEPS:
            if m == 0:
                copies = send_field(rv.at[m], 2 * m + 2)
                unsent += [functools.partial(when, exists[j], c.wait_send) for j, c in copies.items()]
                send_basis(4)
            else:
                copies = None
                for j in NEAR:
                    far_r[j] = far_residual(j, product_copies, scale, wide)
            span_copies = send_span(rv.at[m], m + 1)
            unsent += [c.wait_send for c in span_copies]
            rr = product(r, r)
        q = r

    n0, n1 = (n / (n + EPSILON) for n in norms)
    cross = across * (1.0 - n0) / jnp.sqrt(norms[1] + EPSILON)
    lane = iota((24, CAP), 1)
    whole = gram_mean + jnp.where((row24 == 20) & (lane == 20), n0, 0.0)
    whole = whole + jnp.where((row24 == 21) & (lane == 21), n1, 0.0)
    whole = whole + jnp.where((row24 + lane == 41) & (row24 >= 20) & (lane >= 20), cross, 0.0)
    c_row = row_of(jnp.where(row24[:, 0:1] < 22, solved, 0.0))
    p_row = value * scale
    p_row = jnp.where(iota((1, CAP), 1) == 21, p_row * scale, p_row)
    inner = jnp.sum(whole * c_row - jnp.where(eye, 2.0 * p_row, 0.0), axis=1, keepdims=True)
    inner = jnp.where(row24[:, 0:1] < 22, inner * solved, 0.0)
    rr = ww * scale * scale + jnp.sum(inner, axis=0, keepdims=True)
    beta = jnp.sqrt(jnp.maximum(rr, 0.0) + EPSILON)
    scale = 1.0 / beta
    nv_ref[STEPS - 1] = jnp.concatenate([x * scale for x in q], axis=0)
    hess[-1] = jnp.where(iota((1, CAP), 1) == 22, beta, hess[-1])
    hess_ref[...] = jnp.concatenate(hess, axis=0)[:, 0:23]

    for j in range(4):
        when(exists[j], first[j].wait_send)
        when(exists[3 - j], messages[j].wait_send)
        when(exists[j], pltpu.make_async_copy(kv, kv, kv_send.at[j]).wait)
    for c in first_span:
        c.wait_send()
    for wait in unsent:
        wait()


def on_device(grid, krylov, limiter, pseudo_diag, face_states, face_angle, face_area, slope_weight,
              span_coupling, face_cells, send_list, send_count):
    ns, ny, nz = grid
    count = float(5 * 4 * CELLS * ns * ny * nz)

    def halves(x):
        lead = x.shape[:-2]
        x = x.reshape(*lead, 4, 2, CAP)
        return jnp.swapaxes(x, -3, -2).reshape(*lead, 8, CAP)

    anywhere = pl.BlockSpec(memory_space=pl.ANY)
    members = ns * ny + nz
    dma = pltpu.SemaphoreType.DMA
    vectors, hess = pl.pallas_call(
        functools.partial(kernel, grid, count),
        out_shape=(
            pltpu.VMEM((STEPS, 40, CAP), F32),
            pltpu.VMEM((STEPS, 23), F32),
        ),
        in_specs=[anywhere] * 10,
        out_specs=(pl.BlockSpec(memory_space=pltpu.VMEM),) * 2,
        scratch_shapes=[
            pltpu.VMEM((NVEC * 40, CAP), F32),
            pltpu.VMEM((5, 8, CAP), F32),
            pltpu.VMEM((8, CAP), F32),
            pltpu.VMEM((2, 5, 4, FACES), F32),
            pltpu.VMEM((1, FACES), F32),
            pltpu.VMEM((1, FACES), F32),
            pltpu.VMEM((1, FACES), F32),
            pltpu.VMEM((1, CELLS), F32),
            pltpu.VMEM((2, FACES), jnp.int32),
            pltpu.VMEM((4, CAP), jnp.int32),
            pltpu.VMEM((5, CELLS, 2 * CELLS), BF16),
            pltpu.VMEM((STEPS, 40, CAP), F32),
            pltpu.VMEM((STEPS, 40, CAP), F32),
            pltpu.VMEM((CELLS, 1536), BF16),
            pltpu.VMEM((CELLS, 2048), BF16),
            pltpu.VMEM((4, CELLS, 2 * CAP), BF16),
            pltpu.VMEM((5, 8, FACES), F32),
            pltpu.VMEM((5, 8, FACES), F32),
            pltpu.VMEM((8, FACES), F32),
            pltpu.VMEM((2, 8, FACES), F32),
            pltpu.VMEM((4, 48, CAP), F32),
            pltpu.VMEM((4, 48, CAP), F32),
            pltpu.VMEM((2 * STEPS, 4, 40, CAP), F32),
            pltpu.VMEM((STEPS, 2, 40, CAP), F32),
            pltpu.VMEM((members, 8, CAP), F32),
            pltpu.VMEM((STEPS, members, 1, CAP), F32),
            dma((10,)),
            dma((4,)),
            dma((4,)),
            dma((2 * STEPS, 4)),
            dma((2 * STEPS, 4)),
            dma((STEPS, 2)),
            dma((STEPS, 2)),
            dma((2,)),
            dma((2,)),
            dma((STEPS, 2)),
            dma((STEPS, 2)),
            pltpu.SemaphoreType.REGULAR,
            pltpu.SemaphoreType.REGULAR,
            pltpu.VMEM((4, NVEC * 40, CAP), F32),
            pltpu.VMEM((40, CAP), F32),
            pltpu.VMEM((4, 40, CAP), F32),
            pltpu.VMEM((4, 40, CAP), F32),
            dma((4,)),
            dma((4,)),
            dma((4,)),
            dma((4,)),
        ],
        compiler_params=pltpu.CompilerParams(
            collective_id=0, has_side_effects=True, vmem_limit_bytes=60 * 2**20
        ),
    )(
        halves(krylov).reshape(NVEC * 40, CAP),
        halves(limiter),
        halves(pseudo_diag),
        face_states,
        face_angle[None],
        face_area[None],
        slope_weight[None],
        span_coupling[None],
        face_cells,
        send_list,
    )
    vectors = jnp.swapaxes(vectors.reshape(STEPS, 5, 2, 4, CAP), 2, 3)
    return vectors.reshape(STEPS, 5, 4, CELLS), hess


def solution(mesh):
    ns, nd = mesh.shape["span"], mesh.shape["dom"]
    ny = 4 if nd >= 16 else 2
    return jax.shard_map(
        functools.partial(on_device, (ns, ny, nd // ny)),
        mesh=mesh,
        in_specs=(
            P(None, None, "span", "dom"),
            P(None, "span", "dom"),
            P("span", "dom"),
            P(None, None, "span", "dom"),
            P("dom"),
            P("dom"),
            P("dom"),
            P("dom"),
            P(None, "dom"),
            P(None, "dom"),
            P(None, "dom"),
        ),
        out_specs=(P(None, None, "span", "dom"), P()),
        check_vma=False,
    )
```

```python
import functools

import jax
import jax.numpy as jnp
from jax import lax
from jax.experimental import pallas as pl
from jax.experimental.pallas import tpu as pltpu
from jax.sharding import PartitionSpec as P

MESH = pl.DeviceIdType.MESH
OFFSETS = (-2, -1, 1, 2)
NEAR = (1, 2, 0, 3)
PACE = (0, 2, 5, 7, 10, 13, 16, 18, 19)
EPSILON = 1e-06
F32 = jnp.float32
BF16 = jnp.bfloat16
STEPS = 3
NVEC = 20
CELLS = 256
FACES = 512
CAP = 128


def dot_nn(a, b):
    return lax.dot_general(a, b, (((1,), (0,)), ((), ())), preferred_element_type=F32)


def dot_nt(a, b):
    return lax.dot_general(a, b, (((1,), (1,)), ((), ())), preferred_element_type=F32)


def iota(shape, dim):
    return lax.broadcasted_iota(jnp.int32, shape, dim)


def top_rows(shape):
    return (iota(shape, 0) & 4) == 0


def flip(x):
    return pltpu.roll(x, 4, 0)


def split2(x):
    hi = x.astype(BF16).astype(F32)
    return jnp.concatenate([hi, x - hi], axis=0)


def split3(x):
    hi = x.astype(BF16).astype(F32)
    rest = x - hi
    mid = rest.astype(BF16).astype(F32)
    return jnp.concatenate([hi, mid, rest - mid], axis=0)


def operand(fields):
    both = split2(jnp.concatenate(fields, axis=0))
    top = top_rows(both.shape)
    return jnp.concatenate([jnp.where(top, both, 0.0), jnp.where(top, 0.0, both)], axis=1).astype(BF16)


def joined(y):
    half = y.shape[0] // 2
    return y[:half] + y[half:]


def packed_cells(y):
    out = []
    for v in range(5):
        low, high = y[8 * v : 8 * v + 8, :CAP], y[8 * v : 8 * v + 8, CAP:]
        top = top_rows(low.shape)
        out.append(jnp.where(top, low, high) + flip(jnp.where(top, high, low)))
    return out


def one_hot(size, row):
    return (iota((size, row.shape[1]), 0) == row).astype(F32)


def kernel(
    grid,
    count,
    k_any,
    lim_any,
    pd_any,
    fs_any,
    angle_any,
    area_any,
    weight_any,
    coupling_any,
    cells_any,
    sl_any,
    nv_ref,
    hess_ref,
    kv,
    limv,
    pdv,
    fsv,
    anglev,
    areav,
    weightv,
    couplingv,
    cellsv,
    slv,
    m_slope,
    sv,
    rv,
    w_own,
    w_sc,
    w_nb,
    cf_int,
    cf_gf,
    pl_int,
    pl_gf,
    msg_out,
    msg_in,
    nbuf,
    sbuf,
    gbuf,
    abuf,
    load_sem,
    msg_send,
    msg_recv,
    nb_send,
    nb_recv,
    sp_send,
    sp_recv,
    g_send,
    g_recv,
    a_send,
    a_recv,
    meet_y,
    meet_z,
    far_kv,
    wv,
    far_w,
    far_r,
    kv_send,
    kv_recv,
    w_send,
    w_recv,
):
    ns, ny, nz = grid
    nd = ny * nz
    s = lax.axis_index("span")
    d = lax.axis_index("dom")
    y, z = d // nz, lax.rem(d, nz)

    def dom_at(offset):
        return lax.rem(d + (offset + nd), nd)

    def span_at(offset):
        return lax.rem(s + (offset + ns), ns)

    xs = ns // 2
    x, core = s // 2, lax.rem(s, 2)
    places = (s * ny + y, z)
    sizes = (ns * ny, nz)
    starts = (0, ns * ny)

    def others(stage):
        if stage:
            hops = sorted(range(1, nz), key=lambda k: -min(k, nz - k))
            return [(s, y * nz + lax.rem(z + k, nz)) for k in hops]
        hops = [(i, c, k) for i in range(xs) for c in range(2) for k in range(ny)]
        hops = sorted(hops, key=lambda h: -(min(h[0], xs - h[0]) + min(h[2], ny - h[2])))
        return [
            (lax.rem(x + i, xs) * 2 + lax.rem(core + c, 2), lax.rem(y + k, ny) * nz + z)
            for i, c, k in hops
            if (i, c, k) != (0, 0, 0)
        ]

    barrier = pltpu.get_barrier_semaphore()
    near_z = [(s, y * nz + lax.rem(z + k, nz)) for k in (nz - 2, nz - 1, 1, 2)]
    near_y = [(s, lax.rem(y + k, ny) * nz + z) for k in range(1, ny)]
    partners = [(s, dom_at(o)) for o in OFFSETS] + near_z + near_y
    partners += [(lax.rem(s + k, ns), d) for k in range(1, ns)]
    for device in partners:
        pl.semaphore_signal(barrier, inc=1, device_id=device, device_id_type=MESH)

    def greet(semaphore, devices):
        for device in devices:
            pl.semaphore_signal(semaphore, inc=1, device_id=device, device_id_type=MESH)

    pairs = (
        (fs_any, fsv),
        (angle_any, anglev),
        (area_any, areav),
        (weight_any, weightv),
        (cells_any, cellsv),
        (sl_any, slv),
        (k_any, kv),
        (coupling_any, couplingv),
        (lim_any, limv),
        (pd_any, pdv),
    )
    loads = [pltpu.make_async_copy(src, dst, load_sem.at[i]) for i, (src, dst) in enumerate(pairs)]
    for load in loads:
        load.start()

    exists = [(d + o >= 0) & (d + o < nd) for o in OFFSETS]
    for j in range(4):

        @pl.when(jnp.logical_not(exists[j]))
        def _():
            msg_in[j] = jnp.zeros((48, CAP), F32)
            for number in range(2 * STEPS):
                nbuf[number, j] = jnp.zeros((40, CAP), F32)
            far_kv[j] = jnp.zeros((NVEC * 40 - 40, CAP), F32)
            far_w[j] = jnp.zeros((40, CAP), F32)

    def when(condition, action):
        @pl.when(condition)
        def _():
            action()

    def send_field(src, number):
        copies = []
        for j in reversed(NEAR):
            copy = pltpu.make_async_remote_copy(
                src_ref=src,
                dst_ref=nbuf.at[number, 3 - j],
                send_sem=nb_send.at[number, j],
                recv_sem=nb_recv.at[number, 3 - j],
                device_id=(s, dom_at(OFFSETS[j])),
                device_id_type=MESH,
            )
            when(exists[j], copy.start)
            copies.append((j, copy))
        return dict(copies)

    def send_span(src, number):
        copies = []
        for side, offset in ((0, 1), (1, -1)):
            copy = pltpu.make_async_remote_copy(
                src_ref=src,
                dst_ref=sbuf.at[number, side],
                send_sem=sp_send.at[number, side],
                recv_sem=sp_recv.at[number, side],
                device_id=(span_at(offset), d),
                device_id_type=MESH,
            )
            copy.start()
            copies.append(copy)
        return copies

    unsent = []

    def send_basis(part):
        low, high = PACE[part], PACE[part + 1]
        rows = pl.ds(40 * low, 40 * (high - low))
        for j in reversed(NEAR):
            copy = pltpu.make_async_remote_copy(
                src_ref=kv.at[rows],
                dst_ref=far_kv.at[3 - j, rows],
                send_sem=kv_send.at[j],
                recv_sem=kv_recv.at[3 - j],
                device_id=(s, dom_at(OFFSETS[j])),
                device_id_type=MESH,
            )
            when(exists[j], copy.start)

    def send_product():
        copies = {}
        for j in reversed(NEAR):
            copies[j] = pltpu.make_async_remote_copy(
                src_ref=wv,
                dst_ref=far_w.at[3 - j],
                send_sem=w_send.at[j],
                recv_sem=w_recv.at[3 - j],
                device_id=(s, dom_at(OFFSETS[j])),
                device_id_type=MESH,
            )
            when(exists[j], copies[j].start)
        return copies


    def sum_start(buf, send, recv, stage, value):
        place = buf.at[starts[stage] + places[stage]]
        buf[pl.ds(starts[stage] + places[stage], 1)] = value[None]
        for device in others(stage):
            pltpu.make_async_remote_copy(
                src_ref=place,
                dst_ref=place,
                send_sem=send.at[stage],
                recv_sem=recv.at[stage],
                device_id=device,
                device_id_type=MESH,
            ).start()
        span = buf.at[pl.ds(starts[stage], sizes[stage] - 1)]
        unsent.append(pltpu.make_async_copy(span, span, send.at[stage]).wait)

    def sum_finish(buf, recv, stage):
        n = sizes[stage]
        span = buf.at[pl.ds(starts[stage], n - 1)]
        pltpu.make_async_copy(span, span, recv.at[stage]).wait()
        terms = [buf[starts[stage] + k] for k in range(n)]
        while len(terms) > 1:
            terms = [sum(terms[i + 1 : i + 2], terms[i]) for i in range(0, len(terms), 2)]
        return terms[0]

    for load in loads[:5]:
        load.wait()
    angle, area, weight = anglev[...], areav[...], weightv[...]
    owner, other = cellsv[0:1, :], cellsv[1:2, :]
    nx, ny_ = jnp.cos(angle), jnp.sin(angle)
    state = [jnp.concatenate([fsv[0, v], fsv[1, v]], axis=0) for v in range(5)]
    inv = 1.0 / state[0]
    u1, u2, u3 = state[1] * inv, state[2] * inv, state[3] * inv
    pressure = 0.4 * (state[4] - 0.5 * (state[1] * u1 + state[2] * u2 + state[3] * u3))
    enthalpy = (state[4] + pressure) * inv
    speed = jnp.abs(u1 * nx + u2 * ny_) + jnp.sqrt(1.4 * pressure * inv)
    lam = jnp.maximum(speed, flip(speed))
    lam = jnp.where(top_rows(lam.shape), lam, -lam)
    half_area = 0.5 * area
    coefs = [u1, u2, u3, enthalpy, lam]
    for i, c in enumerate(coefs):
        cf_int[i] = c
    inside = (other < CELLS).astype(F32)
    pl_int[0:1, :] = nx
    pl_int[1:2, :] = ny_
    pl_int[2:3, :] = half_area * inside
    pl_int[3:4, :] = weight * inside
    pl_int[4:8, :] = jnp.zeros((4, FACES), F32)

    loads[5].wait()
    plane_rows = jnp.concatenate(
        [nx, ny_, half_area, weight, owner.astype(F32), jnp.zeros((3, FACES), F32)], axis=0
    )
    gathered = split3(jnp.concatenate([*coefs, plane_rows], axis=0)).astype(BF16)
    for j in range(4):
        slots = (iota((CAP, FACES), 0) + (CELLS + j * CAP) == other).astype(F32).astype(BF16)
        part = dot_nt(gathered, slots)
        part = part[0:48] + part[48:96] + part[96:144]
        msg_out[j, 0:45, :] = part[0:45]
        msg_out[j, 45:46, :] = slv[3 - j : 4 - j, :].astype(F32)
        msg_out[j, 46:48, :] = jnp.zeros((2, CAP), F32)

    pl.semaphore_wait(barrier, len(partners))

    first = send_field(k_any.at[pl.ds(40 * NVEC - 40, 40)], 0)
    messages = {}
    for j in reversed(NEAR):
        copy = pltpu.make_async_remote_copy(
            src_ref=msg_out.at[j],
            dst_ref=msg_in.at[j],
            send_sem=msg_send.at[j],
            recv_sem=msg_recv.at[j],
            device_id=(s, dom_at(OFFSETS[3 - j])),
            device_id_type=MESH,
        )
        when(exists[3 - j], copy.start)
        messages[j] = copy
    first_span = send_span(k_any.at[pl.ds(40 * NVEC - 40, 40)], 0)
    circle = near_y + [near_z[0], near_z[3]]
    greet(meet_y, circle)

    loads[6].wait()
    send_basis(0)
    total = jnp.zeros((72, 72), F32)
    for pair in range(20):
        rows = jnp.concatenate(
            [kv[pl.ds(2 * pair + i, NVEC, stride=40), :] for i in range(2)], axis=1
        )
        rows = jnp.concatenate([rows, jnp.zeros((4, 2 * CAP), F32)], axis=0)
        rows = split3(rows).astype(BF16)
        total = total + dot_nt(rows, rows)
    rows = total[0:24] + total[24:48] + total[48:72]
    gram = rows[:, 0:24] + rows[:, 24:48] + rows[:, 48:72]
    gram = jnp.concatenate([gram, jnp.zeros((24, CAP - 24), F32)], axis=1)
    gram = gram[0:8] + pltpu.roll(gram[8:16], 32, 1) + pltpu.roll(gram[16:24], 64, 1)

    hot_a, hot_b = one_hot(CELLS, owner), one_hot(CELLS, other)
    w_own[:, 0:512] = (hot_a - hot_b).astype(BF16)
    w_sc[:, 0:512] = hot_a.astype(BF16)
    w_sc[:, 512:1024] = hot_b.astype(BF16)
    for j in range(4):
        at = 512 + j * CAP
        hot = one_hot(CELLS, msg_out[j, 44:45, :].astype(jnp.int32)).astype(BF16)
        w_own[:, at : at + CAP] = hot
        w_sc[:, at + 512 : at + 512 + CAP] = hot
        hot = one_hot(CELLS, slv[j : j + 1, :])
        w_own[:, at + 512 : at + 512 + CAP] = (-hot).astype(BF16)
        w_sc[:, at + 1024 : at + 1024 + CAP] = hot.astype(BF16)

    def near(own):
        return joined(dot_nn(operand(own), w_own[...]))

    first_near = near([kv[40 * NVEC - 40 :, :]])

    pl.semaphore_wait(meet_y, len(circle))
    far_z = [(s, y * nz + lax.rem(z + k, nz)) for k in (4, nz - 4)] if nz > 8 else []
    greet(meet_z, far_z)
    sum_start(gbuf, g_send, g_recv, 0, gram)

    for j in NEAR:
        when(exists[j], messages[j].wait_recv)
        at = j * CAP
        for i in range(5):
            mine, theirs = msg_out[j, 8 * i : 8 * i + 8, :], msg_in[j, 8 * i : 8 * i + 8, :]
            cf_gf[i, :, at : at + CAP] = jnp.where(top_rows(mine.shape), mine, theirs)
        for side, msg in ((0, msg_out), (1, msg_in)):
            pl_gf[side, :, at : at + CAP] = msg[j, 40:48, :]
        w_nb[j, :, 0:CAP] = (-one_hot(CELLS, msg_in[j, 45:46, :].astype(jnp.int32))).astype(BF16)
        w_nb[j, :, CAP:] = one_hot(CELLS, msg_in[j, 44:45, :].astype(jnp.int32)).astype(BF16)

    def jumps(near, number, copies):
        ghost = [None] * 4
        foreign = [None] * 4
        for j in NEAR:
            if copies is None:
                block = far_r[j]
            else:
                when(exists[j], copies[3 - j].wait_recv)
                block = nbuf[number, j]
            part = joined(dot_nn(operand([block]), w_nb[j]))
            ghost[3 - j] = part[:, :CAP]
            foreign[j] = part[:, CAP:]
        return (
            near[:, 0:512],
            near[:, 512:1024] + jnp.concatenate(ghost, axis=1),
            near[:, 1024:1536] + jnp.concatenate(foreign, axis=1),
        )

    def transposed(e, cf, nx, ny, half_area):
        e = [half_area * x for x in e]
        u1, u2, u3, enthalpy, lam = (cf[i] for i in range(5))
        vn = u1 * nx + u2 * ny
        phi = 0.2 * (u1 * u1 + u2 * u2 + u3 * u3)
        cp = e[1] * nx + e[2] * ny + e[4] * vn
        ch = e[0] + e[1] * u1 + e[2] * u2 + e[3] * u3 + e[4] * enthalpy
        diag = vn + lam
        cp4 = 0.4 * cp
        return [
            e[0] * diag + cp * phi - ch * vn,
            e[1] * diag - u1 * cp4 + ch * nx,
            e[2] * diag - u2 * cp4 + ch * ny,
            e[3] * diag - u3 * cp4,
            e[4] * diag + cp4,
        ]

    def state_part(near, number, copies):
        e_int, e_gh, e_for = jumps(near, number, copies)
        jump_int, jump_gf = [], []
        for v in range(5):
            x = e_int[8 * v : 8 * v + 8]
            jump_int.append(x + flip(x))
            g, f = e_gh[8 * v : 8 * v + 8], e_for[8 * v : 8 * v + 8]
            top = top_rows(g.shape)
            jump_gf.append(jnp.where(top, g, f) + flip(jnp.where(top, f, g)))
        g_int = transposed(jump_int, cf_int, pl_int[0:1, :], pl_int[1:2, :], pl_int[2:3, :])
        top = top_rows((8, FACES))
        rows = [jnp.where(top, pl_gf[0, i : i + 1, :], pl_gf[1, i : i + 1, :]) for i in range(3)]
        g_gf = transposed(jump_gf, cf_gf, *rows)
        parts = []
        for g in (jnp.concatenate(g_int, axis=0), jnp.concatenate(g_gf, axis=0)):
            top = top_rows(g.shape)
            parts += [jnp.where(top, g, 0.0), jnp.where(top, 0.0, g)]
        lhs = split2(jnp.concatenate(parts, axis=1)).astype(BF16)
        return packed_cells(joined(dot_nt(lhs, w_sc[...])))

    def slope_matrices():
        def store(index, faces, weights, cells):
            hi = weights.astype(BF16)
            lo = (weights - hi.astype(F32)).astype(BF16)
            matrix = dot_nt(faces * hi, cells) + dot_nt(faces * lo, cells)
            hi = matrix.astype(BF16)
            m_slope[index, :, 0:CELLS] = hi
            m_slope[index, :, CELLS:] = (matrix - hi.astype(F32)).astype(BF16)

        for j in range(4):
            g, f = (3 - j) * CAP, j * CAP
            weights = jnp.concatenate([pl_gf[0, 3:4, g : g + CAP], pl_gf[1, 3:4, f : f + CAP]], axis=1)
            cells = jnp.concatenate(
                [w_own[:, 512 + g : 512 + g + CAP], w_own[:, 1024 + f : 1024 + f + CAP]], axis=1
            )
            store(j, w_nb[j], weights, cells)
        weights = jnp.concatenate([pl_int[3:4, :], pl_gf[0, 3:4, :], pl_gf[1, 3:4, :]], axis=1)
        store(4, w_own[...], weights, w_own[...])

    def slope_near(own):
        return dot_nn(operand(own), m_slope[4])

    def slope_part(total, number, copies):
        for j in NEAR:
            when(exists[j], copies[3 - j].wait_recv)
            total = total + dot_nn(operand([nbuf[number, j]]), m_slope[j])
        total = joined(total)
        return packed_cells(total[:, :CELLS] + total[:, CELLS:])

    def far_residual(j, copies, scale, wide):
        when(exists[j], copies[3 - j].wait_recv)
        arrived = pltpu.make_async_copy(far_kv.at[j], far_kv.at[j], kv_recv.at[j])
        when(exists[j], arrived.wait)
        out = []
        for v in range(5):
            rows = slice(8 * v, 8 * v + 8)
            r = far_w[j, rows, :] * scale
            for i in range(NVEC - 1):
                r = r - wide[i : i + 1, :] * far_kv[j, 40 * i + 8 * v : 40 * i + 8 * v + 8, :]
            r = r - wide[NVEC - 1 : NVEC, :] * nbuf[0, j, rows, :]
            out.append(r - wide[NVEC : NVEC + 1, :] * (nbuf[2, j, rows, :] * scale))
        return jnp.concatenate(out, axis=0)

    row = iota((8, CAP), 0)
    layer = row & 3
    loads[7].wait()
    coupling = jnp.where(row < 4, couplingv[:, 0:CAP], couplingv[:, CAP:])
    eye = iota((24, CAP), 0) == iota((24, CAP), 1)
    row24 = iota((24, CAP), 0)

    def row_of(column):
        return jnp.sum(jnp.where(eye, column, 0.0), axis=0, keepdims=True)

    def local_sums(terms):
        rows = []
        for i in range(24):
            if i in terms:
                rows.append(jnp.sum(terms[i], axis=0, keepdims=True))
            else:
                rows.append(jnp.zeros((1, CAP), F32))
        return row_of(jnp.sum(jnp.concatenate(rows, axis=0), axis=1, keepdims=True))

    def product(a, b):
        out = a[0] * b[0]
        for v in range(1, 5):
            out = out + a[v] * b[v]
        return out

    def basis(i):
        return [kv[40 * i + 8 * v : 40 * i + 8 * v + 8, :] for v in range(5)]

    q = basis(NVEC - 1)
    copies, span_copies = first, first_span
    inverse = None
    done = []
    rr = None
    hess = []
    norms = []
    for m in range(STEPS):
        state_terms = state_part(near(q) if m else first_near, 2 * m, copies)
        if m == 0:
            loads[8].wait()
            loads[9].wait()
        slope_field = [limv[v] * state_terms[v] for v in range(5)]
        sv[m] = jnp.concatenate(slope_field, axis=0)
        slope_copies = send_field(sv.at[m], 2 * m + 1)
        if m < 2:
            send_basis(4 * m + 1)
        if m == 0:
            slope_matrices()
            gram = sum_finish(gbuf, g_recv, 0)
            if far_z:
                pl.semaphore_wait(meet_z, len(far_z))
            sum_start(gbuf, g_send, g_recv, 1, gram)
        slope_own = slope_near(slope_field)
        for copy in span_copies:
            copy.wait_recv()
        local = []
        for v in range(5):
            above = jnp.where(layer == 0, pltpu.roll(sbuf[m, 0, 8 * v : 8 * v + 8, :], 5, 0), pltpu.roll(q[v], 1, 0))
            below = jnp.where(layer == 3, pltpu.roll(sbuf[m, 1, 8 * v : 8 * v + 8, :], 3, 0), pltpu.roll(q[v], 7, 0))
            local.append(
                pdv[...] * q[v] + coupling * (2.0 * q[v] - above - below) + state_terms[v]
            )
        slope_terms = slope_part(slope_own, 2 * m + 1, slope_copies)
        w = [local[v] - slope_terms[v] for v in range(5)]

        terms = {i: product(basis(i), w) for i in range(NVEC)}
        for i, vector in enumerate(done):
            terms[NVEC + i] = product(vector, w)
        if m:
            terms[NVEC + m - 1] = product(q, w)
            terms[22] = rr
        if m == STEPS - 1:
            terms[23] = product(w, w)
        value = local_sums(terms)
        sum_start(abuf.at[m], a_send.at[m], a_recv.at[m], 0, value)
        if m == 1:
            wv[...] = jnp.concatenate(w, axis=0)
            product_copies = send_product()
            unsent += [functools.partial(when, exists[j], c.wait_send) for j, c in product_copies.items()]
        if m < 2:
            send_basis(4 * m + 2)
        value = sum_finish(abuf.at[m], a_recv.at[m], 0)
        sum_start(abuf.at[m], a_send.at[m], a_recv.at[m], 1, value)
        if m < 2:
            send_basis(4 * m + 3)
        if m == 0:
            gram = sum_finish(gbuf, g_recv, 1) / count
            wide = jnp.concatenate(
                [gram, pltpu.roll(gram, CAP - 32, 1), pltpu.roll(gram, CAP - 64, 1)], axis=0
            )
            lane = iota((24, CAP), 1)
            kept = (lane < NVEC) & (row24 < NVEC)
            diagonal = (row24 == lane) & (row24 >= NVEC)
            gram_mean = jnp.where(kept, wide, 0.0)
            work = gram_mean + jnp.where(diagonal | (lane == row24 + 32), 1.0, 0.0)
            for k in range(NVEC):
                column = jnp.sum(jnp.where(lane == k, work, 0.0), axis=1, keepdims=True)
                pivot = work[k : k + 1, :]
                scale = 1.0 / column[k : k + 1, :]
                work = work - (column - jnp.where(row24[:, 0:1] == k, 1.0, 0.0)) * (pivot * scale)
            inverse = pltpu.roll(work, CAP - 32, 1)
        value = sum_finish(abuf.at[m], a_recv.at[m], 1)
        value = value / count
        solved = jnp.sum(inverse * value, axis=1, keepdims=True)
        if m:
            norms.append(solved[22:23, :])
            ww = solved[23:24, :]
            beta = jnp.sqrt(norms[-1] + EPSILON)
            scale = 1.0 / beta
            last = [x * scale for x in q]
            nv_ref[m - 1] = jnp.concatenate(last, axis=0)
            done.append(last)
            hess[-1] = jnp.where(iota((1, CAP), 1) == 22, beta, hess[-1])
            w = [x * scale for x in w]
            solved = solved * scale
            solved = jnp.where(row24[:, 0:1] == NVEC + m - 1, solved * scale, solved)
            if m == 1:
                across = solved[20:21, :]
        hess.append(jnp.where(iota((1, CAP), 1) < NVEC + m, row_of(solved), 0.0))
        wide = jnp.broadcast_to(solved, (24, CAP))
        r = w
        for i in range(NVEC + m):
            c = wide[i : i + 1, :]
            vector = basis(i) if i < NVEC else done[i - NVEC]
            r = [r[v] - c * vector[v] for v in range(5)]
        rv[m] = jnp.concatenate(r, axis=0)
        unsent += [functools.partial(when, exists[j], c.wait_send) for j, c in slope_copies.items()]
        if m + 1 < STEPS:
            if m == 0:
                copies = send_field(rv.at[m], 2 * m + 2)
                unsent += [functools.partial(when, exists[j], c.wait_send) for j, c in copies.items()]
                send_basis(4)
            else:
                copies = None
                for j in NEAR:
                    far_r[j] = far_residual(j, product_copies, scale, wide)
            span_copies = send_span(rv.at[m], m + 1)
            unsent += [c.wait_send for c in span_copies]
            rr = product(r, r)
        q = r

    n0, n1 = (n / (n + EPSILON) for n in norms)
    cross = across * (1.0 - n0) / jnp.sqrt(norms[1] + EPSILON)
    lane = iota((24, CAP), 1)
    whole = gram_mean + jnp.where((row24 == 20) & (lane == 20), n0, 0.0)
    whole = whole + jnp.where((row24 == 21) & (lane == 21), n1, 0.0)
    whole = whole + jnp.where((row24 + lane == 41) & (row24 >= 20) & (lane >= 20), cross, 0.0)
    c_row = row_of(jnp.where(row24[:, 0:1] < 22, solved, 0.0))
    p_row = value * scale
    p_row = jnp.where(iota((1, CAP), 1) == 21, p_row * scale, p_row)
    inner = jnp.sum(whole * c_row - jnp.where(eye, 2.0 * p_row, 0.0), axis=1, keepdims=True)
    inner = jnp.where(row24[:, 0:1] < 22, inner * solved, 0.0)
    rr = ww * scale * scale + jnp.sum(inner, axis=0, keepdims=True)
    beta = jnp.sqrt(jnp.maximum(rr, 0.0) + EPSILON)
    scale = 1.0 / beta
    nv_ref[STEPS - 1] = jnp.concatenate([x * scale for x in q], axis=0)
    hess[-1] = jnp.where(iota((1, CAP), 1) == 22, beta, hess[-1])
    hess_ref[...] = jnp.concatenate(hess, axis=0)[:, 0:23]

    for j in range(4):
        when(exists[j], first[j].wait_send)
        when(exists[3 - j], messages[j].wait_send)
        sent = kv.at[pl.ds(0, NVEC * 40 - 40)]
        when(exists[j], pltpu.make_async_copy(sent, sent, kv_send.at[j]).wait)
    for c in first_span:
        c.wait_send()
    for wait in unsent:
        wait()


def on_device(grid, krylov, limiter, pseudo_diag, face_states, face_angle, face_area, slope_weight,
              span_coupling, face_cells, send_list, send_count):
    ns, ny, nz = grid
    count = float(5 * 4 * CELLS * ns * ny * nz)

    def halves(x):
        lead = x.shape[:-2]
        x = x.reshape(*lead, 4, 2, CAP)
        return jnp.swapaxes(x, -3, -2).reshape(*lead, 8, CAP)

    anywhere = pl.BlockSpec(memory_space=pl.ANY)
    members = ns * ny + nz
    dma = pltpu.SemaphoreType.DMA
    vectors, hess = pl.pallas_call(
        functools.partial(kernel, grid, count),
        out_shape=(
            pltpu.VMEM((STEPS, 40, CAP), F32),
            pltpu.VMEM((STEPS, 23), F32),
        ),
        in_specs=[anywhere] * 10,
        out_specs=(pl.BlockSpec(memory_space=pltpu.VMEM),) * 2,
        scratch_shapes=[
            pltpu.VMEM((NVEC * 40, CAP), F32),
            pltpu.VMEM((5, 8, CAP), F32),
            pltpu.VMEM((8, CAP), F32),
            pltpu.VMEM((2, 5, 4, FACES), F32),
            pltpu.VMEM((1, FACES), F32),
            pltpu.VMEM((1, FACES), F32),
            pltpu.VMEM((1, FACES), F32),
            pltpu.VMEM((1, CELLS), F32),
            pltpu.VMEM((2, FACES), jnp.int32),
            pltpu.VMEM((4, CAP), jnp.int32),
            pltpu.VMEM((5, CELLS, 2 * CELLS), BF16),
            pltpu.VMEM((STEPS, 40, CAP), F32),
            pltpu.VMEM((STEPS, 40, CAP), F32),
            pltpu.VMEM((CELLS, 1536), BF16),
            pltpu.VMEM((CELLS, 2048), BF16),
            pltpu.VMEM((4, CELLS, 2 * CAP), BF16),
            pltpu.VMEM((5, 8, FACES), F32),
            pltpu.VMEM((5, 8, FACES), F32),
            pltpu.VMEM((8, FACES), F32),
            pltpu.VMEM((2, 8, FACES), F32),
            pltpu.VMEM((4, 48, CAP), F32),
            pltpu.VMEM((4, 48, CAP), F32),
            pltpu.VMEM((2 * STEPS, 4, 40, CAP), F32),
            pltpu.VMEM((STEPS, 2, 40, CAP), F32),
            pltpu.VMEM((members, 8, CAP), F32),
            pltpu.VMEM((STEPS, members, 1, CAP), F32),
            dma((10,)),
            dma((4,)),
            dma((4,)),
            dma((2 * STEPS, 4)),
            dma((2 * STEPS, 4)),
            dma((STEPS, 2)),
            dma((STEPS, 2)),
            dma((2,)),
            dma((2,)),
            dma((STEPS, 2)),
            dma((STEPS, 2)),
            pltpu.SemaphoreType.REGULAR,
            pltpu.SemaphoreType.REGULAR,
            pltpu.VMEM((4, NVEC * 40 - 40, CAP), F32),
            pltpu.VMEM((40, CAP), F32),
            pltpu.VMEM((4, 40, CAP), F32),
            pltpu.VMEM((4, 40, CAP), F32),
            dma((4,)),
            dma((4,)),
            dma((4,)),
            dma((4,)),
        ],
        compiler_params=pltpu.CompilerParams(
            collective_id=0, has_side_effects=True, vmem_limit_bytes=60 * 2**20
        ),
    )(
        halves(krylov).reshape(NVEC * 40, CAP),
        halves(limiter),
        halves(pseudo_diag),
        face_states,
        face_angle[None],
        face_area[None],
        slope_weight[None],
        span_coupling[None],
        face_cells,
        send_list,
    )
    vectors = jnp.swapaxes(vectors.reshape(STEPS, 5, 2, 4, CAP), 2, 3)
    return vectors.reshape(STEPS, 5, 4, CELLS), hess


def solution(mesh):
    ns, nd = mesh.shape["span"], mesh.shape["dom"]
    ny = 4 if nd >= 16 else 2
    return jax.shard_map(
        functools.partial(on_device, (ns, ny, nd // ny)),
        mesh=mesh,
        in_specs=(
            P(None, None, "span", "dom"),
            P(None, "span", "dom"),
            P("span", "dom"),
            P(None, None, "span", "dom"),
            P("dom"),
            P("dom"),
            P("dom"),
            P("dom"),
            P(None, "dom"),
            P(None, "dom"),
            P(None, "dom"),
        ),
        out_specs=(P(None, None, "span", "dom"), P()),
        check_vma=False,
    )
```
